512 devices in a mesh: gx: 64 (over y, z), gy: 8 (over x, core).
Axes of the slice: x: 4, y: 4, z: 16, core: 2. Of those that a mesh axis runs over, the one named last changes fastest.
Arguments:
- source: float32 [8, 2048, 2048], P(None, 'gx', 'gy'), may hold values from -6 to 6
- kappa_sq: bfloat16 [8, 2048, 2048], P(None, 'gx', 'gy'), may hold values from 0.0039978027 to 0.079589844
- face_x: bfloat16 [8, 2048, 2048], P(None, 'gx', 'gy'), may hold values from 0.25 to 1
- face_y: bfloat16 [8, 2048, 2048], P(None, 'gx', 'gy'), may hold values from 0.25 to 1
- face_z: bfloat16 [8, 2048, 2048], P(None, 'gx', 'gy'), may hold values from 0.0049743652 to 0.049804688
Outputs:
- field: float32 [8, 2048, 2048], P(None, 'gx', 'gy')
The draws below stay inside these ranges and needn't reach their ends.
All inputs are finite; a program needn't handle non-finite values.
Results may differ from the reference program's by a relative error of at most 0.0003.
Values sent between devices are 32-bit elements; how exact they have to be, the bound alone decides.
A program may use at most 64 MiB of HBM per device.

```python
import math
import jax
import jax.numpy as jnp
from jax import lax

NZ = 8
LEVELS = 5
COARSE_SWEEPS = 4
NX = 2048
NY = 2048


def draw_source(key, part):
    key = jax.random.fold_in(key, 7)
    return jnp.clip(jax.random.normal(key, (NZ, NX, NY), jnp.float32), -6.0, 6.0)


def shard_levels(rng, shape, pieces, smallest, top_value):
    def one(axis_at, shards_of):
        draws = jax.random.uniform(jax.random.fold_in(jax.random.fold_in(rng, 6), axis_at), (shards_of,), jnp.float32, smallest / len(pieces), top_value / len(pieces))
        return jnp.repeat(jnp.exp(draws), shape[axis_at] // shards_of).reshape((-1,) + (1,) * (len(shape) - axis_at - 1))

    level = one(*pieces[0])
    for cut in pieces[1:]:
        level = level * one(*cut)
    return level


def setup_inputs(seed: int = 0) -> dict:
    arg_keys = jax.random.split(jax.random.key(seed), 6)
    return {
        "source": draw_source(jax.random.fold_in(arg_keys[5], 71), 0),
        "kappa_sq": jnp.clip(jnp.exp(math.log(0.079589844) - 2.9911416 * jax.random.uniform(arg_keys[1], (NZ, NX, NY), jnp.float32) ** shard_levels(arg_keys[1], (NZ, NX, NY), ((1, 64), (2, 8)), -0.2, 0.2)), 0.0039978027, 0.079589844).astype(jnp.bfloat16),
        "face_x": jnp.clip(jnp.exp(math.log(1.0) - 1.3862944 * jax.random.uniform(arg_keys[2], (NZ, NX, NY), jnp.float32) ** shard_levels(arg_keys[2], (NZ, NX, NY), ((1, 64), (2, 8)), -0.2, 0.2)), 0.25, 1.0).astype(jnp.bfloat16),
        "face_y": jnp.clip(jnp.exp(math.log(1.0) - 1.3862944 * jax.random.uniform(arg_keys[3], (NZ, NX, NY), jnp.float32) ** shard_levels(arg_keys[3], (NZ, NX, NY), ((1, 64), (2, 8)), -0.2, 0.2)), 0.25, 1.0).astype(jnp.bfloat16),
        "face_z": jnp.clip(jnp.exp(math.log(0.049804688) - 2.3038113 * jax.random.uniform(arg_keys[4], (NZ, NX, NY), jnp.float32) ** shard_levels(arg_keys[4], (NZ, NX, NY), ((1, 64), (2, 8)), -0.2, 0.2)), 0.0049743652, 0.049804688).astype(jnp.bfloat16),
    }


DAMPING = 0.8


def lower_cells(values, which_axis):
    padded = jnp.pad(values, [(1, 0) if dimension == which_axis else (0, 0) for dimension in range(3)])
    return lax.slice_in_dim(padded, 0, values.shape[which_axis], axis=which_axis)


def upper_cells(values, which_axis):
    padded = jnp.pad(values, [(0, 1) if dimension == which_axis else (0, 0) for dimension in range(3)])
    return lax.slice_in_dim(padded, 1, values.shape[which_axis] + 1, axis=which_axis)


def restrict(values):
    layer_count, row_count, col_count = values.shape
    blocks = values.astype(jnp.float32).reshape(layer_count, row_count // 2, 2, col_count // 2, 2)
    return (blocks[:, :, 0, :, 0] + blocks[:, :, 0, :, 1] + blocks[:, :, 1, :, 0] + blocks[:, :, 1, :, 1]) * 0.25


def coarsen(coefficients):
    kappa_sq, face_x, face_y, face_z = coefficients
    face_x = face_x.astype(jnp.float32)
    face_y = face_y.astype(jnp.float32)
    coarse_x = (face_x[:, 1::2, 0::2] + face_x[:, 1::2, 1::2]) * 0.25
    coarse_y = (face_y[:, 0::2, 1::2] + face_y[:, 1::2, 1::2]) * 0.25
    return (restrict(kappa_sq), coarse_x, coarse_y, restrict(face_z))


def prolong(values):
    return jnp.repeat(jnp.repeat(values, 2, axis=1), 2, axis=2)


def diagonal_of(coefficients):
    kappa_sq, face_x, face_y, face_z = coefficients
    diagonal = kappa_sq.astype(jnp.float32) + face_x.astype(jnp.float32) + lower_cells(face_x, 1).astype(jnp.float32)
    diagonal = diagonal + face_y.astype(jnp.float32) + lower_cells(face_y, 2).astype(jnp.float32)
    return diagonal + face_z.astype(jnp.float32) + lower_cells(face_z, 0).astype(jnp.float32)


def apply_operator(values, coefficients, diagonal):
    kappa_sq, face_x, face_y, face_z = coefficients
    beside_all = face_x * upper_cells(values, 1) + lower_cells(face_x, 1) * lower_cells(values, 1)
    beside_all = beside_all + face_y * upper_cells(values, 2) + lower_cells(face_y, 2) * lower_cells(values, 2)
    beside_all = beside_all + face_z * upper_cells(values, 0) + lower_cells(face_z, 0) * lower_cells(values, 0)
    return diagonal * values - beside_all


def solve_level(level_index, right_side, hierarchy):
    coefficients = hierarchy[level_index]
    diagonal = diagonal_of(coefficients)

    def relax_once(values):
        return values + DAMPING * (right_side - apply_operator(values, coefficients, diagonal)) / diagonal

    values = DAMPING * right_side / diagonal
    if level_index == LEVELS:
        for sweep_index in range(COARSE_SWEEPS - 1):
            values = relax_once(values)
        return values
    values = relax_once(values)
    residual = right_side - apply_operator(values, coefficients, diagonal)
    correction = solve_level(level_index + 1, restrict(residual), hierarchy)
    values = values + prolong(correction)
    return relax_once(relax_once(values))


def reference(source, kappa_sq, face_x, face_y, face_z):
    hierarchy = [(kappa_sq, face_x, face_y, face_z)]
    for level_index in range(LEVELS):
        hierarchy.append(coarsen(hierarchy[-1]))
    return solve_level(0, source, hierarchy)
```

```python
import jax
import jax.numpy as jnp
from jax import lax
from jax.experimental import pallas as pl
from jax.experimental.pallas import tpu as pltpu
from jax.sharding import PartitionSpec as P

DAMPING = 0.8
F32 = jnp.float32
MESH = pl.DeviceIdType.MESH
NZ, R0, C0 = 8, 32, 256
OWN = (4, 16, 8, 4, 12, 6)
ROWS = (40, 48, 24, 12, 26, 12)
LANES = (384, 256, 128, 128, 128, 128)
REACH = 6


def lanes_of(shape):
    return lax.broadcasted_iota(jnp.int32, shape, len(shape) - 1)


def left(values):
    return pltpu.roll(values, values.shape[-1] - 1, values.ndim - 1)


def right(values):
    return pltpu.roll(values, 1, values.ndim - 1)


def above(values):
    return pltpu.roll(values, values.shape[-2] - 1, values.ndim - 2)


def below(values):
    return pltpu.roll(values, 1, values.ndim - 2)


def take(values, index):
    rows = values.size // 128
    flat = jnp.take_along_axis(values.reshape(rows, 128), jnp.broadcast_to(index, (rows, 128)), axis=1)
    return flat.reshape(values.shape)


def squeeze(first, second, odd=False):
    lane = lanes_of((1, 128))
    index = (2 * lane + (1 if odd else 0)) & 127
    one = take(first, index)
    if second is None:
        return one
    return jnp.where(lanes_of(first.shape) < 64, one, take(second, index))


def pair(values):
    return values + pltpu.roll(values, 127, values.ndim - 1)


def squeeze_wide(values, odd=False, sums=True):
    parts = [values[..., 128 * j : 128 * j + 128] for j in range(values.shape[-1] // 128)]
    if sums:
        parts = [pair(p) for p in parts]
    return squeeze(parts[0], parts[1] if len(parts) > 1 else None, odd)


def stretch_index(kind):
    lane = lanes_of((1, 128))
    half = lane // 2
    if kind == "low":
        return half
    if kind == "high":
        return half + 64
    split = 64 if kind == "ends" else 96
    return half + jnp.where(lane >= split, 64, 0)


def chunks(lo, hi, step, body):
    whole = (hi - lo) // step
    if whole > 1:
        lax.fori_loop(0, whole, lambda n, c: (body(lo + n * step, step), c)[1], 0)
    elif whole == 1:
        body(lo, step)
    if (hi - lo) % step:
        body(lo + whole * step, (hi - lo) % step)


class Level:
    def __init__(self, level, a, d, rd, va, vb):
        self.level, self.a, self.d, self.rd, self.va, self.vb = level, a, d, rd, va, vb
        self.own = OWN[level]
        self.step = (4, 4, 8, 8, 8, 8)[level]

    def rows(self, ref, i, k):
        return ref[pl.ds(i + self.own, k)]

    def field(self, f, i, k):
        return self.a[f, pl.ds(i + self.own, k)]

    def diagonal(self, lo, hi):
        def body(i, k):
            kappa = self.field(1, i, k)
            fx, fxl, fy, fz = self.field(2, i, k), self.field(2, i - 1, k), self.field(3, i, k), self.field(4, i, k)
            d = kappa + fx + fxl + fy + right(fy) + fz + below(fz)
            self.d[pl.ds(i + self.own, k)] = d
            self.rd[pl.ds(i + self.own, k)] = jnp.where(kappa > 0, DAMPING / d, 0.0)

        chunks(lo, hi, self.step, body)

    def beside(self, v, i, k):
        c = self.rows(v, i, k)
        fx, fxl, fy, fz = self.field(2, i, k), self.field(2, i - 1, k), self.field(3, i, k), self.field(4, i, k)
        total = fx * self.rows(v, i + 1, k) + fxl * self.rows(v, i - 1, k)
        total = total + fy * left(c) + right(fy * c)
        total = total + fz * above(c) + below(fz * c)
        return c, total

    def first(self, lo, hi, out):
        def body(i, k):
            out[pl.ds(i + self.own, k)] = self.rows(self.rd, i, k) * self.field(0, i, k)

        chunks(lo, hi, self.step, body)

    def sweep(self, lo, hi, v, out):
        def body(i, k):
            c, total = self.beside(v, i, k)
            new = (1 - DAMPING) * c + self.rows(self.rd, i, k) * (self.field(0, i, k) + total)
            out[pl.ds(i + self.own, k)] = new

        chunks(lo, hi, self.step, body)

    def restrict_residual(self, lo, hi, v, coarse):
        def body(n, m):
            k = 2 * m
            i = 2 * n
            c, total = self.beside(v, i, k)
            residual = self.field(0, i, k) - self.rows(self.d, i, k) * c + total
            residual = residual[..., : min(residual.shape[-1], 256)]
            residual = residual.reshape(m, 2, *residual.shape[1:])
            coarse.a[0, pl.ds(n + coarse.own, m)] = fit(squeeze_wide(residual[:, 0] + residual[:, 1]) * 0.25, coarse)

        chunks(lo // 2, hi // 2, self.step // 2, body)

    def coarsen(self, lo, hi, coarse, fx_low=None):
        def body(n, m):
            both = [self.field(f, 2 * n, 2 * m)[..., : min(self.a.shape[-1], 256)] for f in (1, 2, 3, 4)]
            both = [b.reshape(m, 2, *b.shape[1:]) for b in both]
            kappa, fx, fy, fz = both
            at = pl.ds(n + coarse.own, m)
            coarse.a[1, at] = fit(squeeze_wide(kappa[:, 0] + kappa[:, 1]) * 0.25, coarse)
            coarse.a[2, at] = fit(squeeze_wide(fx[:, 1]) * 0.25, coarse)
            coarse.a[3, at] = fit(squeeze_wide(fy[:, 0] + fy[:, 1], odd=True, sums=False) * 0.25, coarse)
            coarse.a[4, at] = fit(squeeze_wide(fz[:, 0] + fz[:, 1]) * 0.25, coarse)

        chunks(lo, hi, self.step // 2, body)
        if fx_low is not None:
            fx = self.field(2, 2 * fx_low + 1, 1)
            coarse.a[2, pl.ds(fx_low + coarse.own, 1)] = squeeze_wide(fx) * 0.25

    def correct(self, lo, hi, v, coarse, c, out):
        def body(n, m):
            values = c[pl.ds(n + coarse.own, m)]
            if self.level == 0:
                first, second = values[..., :128], values[..., 128:]
                fine = [take(first, stretch_index("low")), take(first, stretch_index("high")), take(second, stretch_index("ends"))]
            elif self.level == 1:
                fine = [take(values, stretch_index("low")), take(values, stretch_index("high"))]
            else:
                fine = [take(values, stretch_index("late"))]
            for j, part in enumerate(fine):
                cols = slice(128 * j, 128 * j + 128)
                at = pl.ds(2 * n + self.own, 2 * m)
                spread = jnp.broadcast_to(part[:, None], (m, 2, NZ, 128)).reshape(2 * m, NZ, 128)
                out[at, :, cols] = v[at, :, cols] + spread

        chunks(lo // 2, hi // 2, max(self.step // 2, 1), body)


def fit(values, coarse):
    if coarse.level == 1:
        return jnp.concatenate([values, jnp.zeros_like(values)], axis=-1)
    return values


def kernel(gx, gy, source, kappa_sq, face_x, face_y, face_z, field, *refs):
    refs = list(refs)

    def get(n):
        out = refs[:n]
        del refs[:n]
        return out

    raw_s, raw_c, wide, out_v = get(4)
    levels = []
    for n in range(6):
        levels.append(Level(n, *get(5)))
    send0, recv0, send1, recv1, sendr, recvr = get(6)
    send4, recv4, wide4, recv4x = get(4)
    sendv, recvv, widev, recvvx, recv3x = get(5)
    load_sem, store_sem, ssem, rsem = get(4)
    l0, l1, l2, l3, l4, l5 = levels

    mx, my = lax.axis_index("gx"), lax.axis_index("gy")

    loads = []
    for h in range(2):
        cols = pl.ds(128 * h, 128)
        loads.append(pltpu.make_async_copy(source.at[:, :, cols], raw_s.at[h], load_sem.at[h, 0]))
        for f, ref in enumerate((kappa_sq, face_x, face_y, face_z)):
            loads.append(pltpu.make_async_copy(ref.at[:, :, cols], raw_c.at[h, f], load_sem.at[h, f + 1]))
    for copy in loads:
        copy.start()

    transfers = {}

    def plan(name, src, dst, dx, dy):
        transfers[name] = (src, dst, dx, dy, len(transfers))

    def there(dx):
        if dx == 0:
            return None
        return mx + dx < gx if dx > 0 else mx + dx >= 0

    def when(cond, action):
        if cond is None:
            action()
        else:
            pl.when(cond)(action)

    def copy_of(name):
        src, dst, dx, dy, n = transfers[name]
        ids = (mx + dx, lax.rem(my + dy + gy, gy))
        return pltpu.make_async_remote_copy(
            src_ref=src, dst_ref=dst, send_sem=ssem.at[n], recv_sem=rsem.at[n], device_id=ids, device_id_type=MESH
        )

    def grouped(names, action, sign):
        by = {}
        for name in names:
            by.setdefault(transfers[name][2], []).append(name)
        for dx, group in by.items():

            def go(group=group):
                for name in group:
                    action(copy_of(name))

            when(there(sign * dx), go)

    def send(names):
        grouped(names, lambda c: c.start(), 1)

    def arrive(names):
        grouped(names, lambda c: c.wait_recv(), -1)

    for d in (1, -1):
        a0, a1 = l0.a, l1.a
        s0, t0 = (33, 1) if d == 1 else (4, 36)
        cols = pl.ds(0, C0)
        plan(("x0", d), a0.at[:, pl.ds(s0, 3), :, cols], a0.at[:, pl.ds(t0, 3), :, cols], d, 0)
        if d == 1:
            plan(("x0f", d), a0.at[2, pl.ds(32, 1), :, cols], a0.at[2, pl.ds(0, 1), :, cols], d, 0)
        cols = pl.ds(0, 128)
        s1, t1, n1 = (17, 1, 15) if d == 1 else (16, 32, 14)
        plan(("x1", d), a1.at[pl.ds(1, 4), pl.ds(s1, n1), :, cols], a1.at[pl.ds(1, 4), pl.ds(t1, n1), :, cols], d, 0)
        s1, t1 = (18, 2) if d == 1 else (16, 32)
        plan(("xr", d), a1.at[0, pl.ds(s1, 14), :, cols], a1.at[0, pl.ds(t1, 14), :, cols], d, 0)
    for dy in (1, -1):
        e = (dy + 1) // 2
        for dx in (-1, 0, 1):
            plan(("y0", dx, dy), send0.at[e], recv0.at[e, dx + 1], dx, dy)
            plan(("y1", dx, dy), send1.at[e], recv1.at[e, dx + 1], dx, dy)
            plan(("yr", dx, dy), sendr.at[e], recvr.at[e, dx + 1], dx, dy)
        plan(("y4", dy), send4, recv4.at[e], 0, dy)
        plan(("yv", dy), sendv, recvv.at[e], 0, dy)
    far = [s * k for k in range(1, REACH + 1) for s in (1, -1)]
    for n, dx in enumerate(far):
        plan(("x4", dx), wide4, recv4x.at[n], dx, 0)
        plan(("xv", dx), widev.at[0], recvvx.at[n], dx, 0)
    for n, dx in enumerate((1, -1)):
        plan(("x3", dx), widev.at[pl.ds(1, 4)], recv3x.at[n], dx, 0)

    def zero(ref, *index):
        ref[index] = jnp.zeros(ref[index].shape, F32)

    @pl.when(mx == 0)
    def _():
        l0.a[:, 0:4] = jnp.zeros((5, 4, NZ, 384), F32)
        l1.a[:, 0:16] = jnp.zeros((5, 16, NZ, 256), F32)
        recv3x[0] = jnp.zeros((4, NZ, 128), F32)

    @pl.when(mx == gx - 1)
    def _():
        l0.a[:, 36:40] = jnp.zeros((5, 4, NZ, 384), F32)
        l1.a[:, 32:48] = jnp.zeros((5, 16, NZ, 256), F32)
        recv3x[1] = jnp.zeros((4, NZ, 128), F32)

    for n, dx in enumerate(far):

        @pl.when(jnp.logical_not(there(-dx)))
        def _(n=n):
            recv4x[n] = jnp.zeros((4, NZ, 128), F32)
            recvvx[n] = jnp.zeros((NZ, 128), F32)

    barrier = pltpu.get_barrier_semaphore()
    partners = [(0, 1), (0, -1)] + [(dx, 0) for dx in far] + [(dx, dy) for dx in (1, -1) for dy in (1, -1)]
    count = 0
    for dx in [0] + far:
        group = [p for p in partners if p[0] == dx]

        def greet(group=group):
            for px, py in group:
                ids = (mx + px, lax.rem(my + py + gy, gy))
                pl.semaphore_signal(barrier, inc=1, device_id=ids, device_id_type=MESH)

        when(there(dx), greet)
        count = count + (len(group) if dx == 0 else jnp.where(there(dx), len(group), 0))

    for copy in loads:
        copy.wait()

    def widen(h, c):
        for f in range(4):
            wide[h, f] = raw_c[h, f].reshape(256, 128).astype(F32)
        top = pl.ds(224, 32)
        wide[h, 0, top] = wide[h, 0, top] + wide[h, 3, top]
        wide[h, 3, top] = jnp.zeros((32, 128), F32)
        return c

    for h in range(2):
        widen(h, 0)

    def turn(i):
        for h in range(2):
            cols = slice(128 * h, 128 * h + 128)
            l0.a[0, 4 + i, :, cols] = raw_s.at[h].reshape(256, 128)[pl.ds(i, NZ, stride=32), :]
            for f in range(4):
                l0.a[1 + f, 4 + i, :, cols] = wide.at[h, f][pl.ds(i, NZ, stride=32), :]

    edge = [0, 1, 2, 28, 29, 30, 31]
    for i in edge:
        turn(i)
    pl.semaphore_wait(barrier, count)
    send([("x0", 1), ("x0f", 1), ("x0", -1)])
    for i in range(3, 28):
        turn(i)

    def pack(a, fields, own, count, width, last, dst):
        per = 128 // width
        lane = lanes_of((NZ, 128))
        for e in range(2):
            at = pl.ds(last, 128) if e == 1 else pl.ds(0, 128)
            for g in range(count // per):
                total = None
                for j in range(per):
                    row = a[fields, own + g * per + j, :, at]
                    shift = (width * j + (width if e == 1 else 0)) % 128
                    row = pltpu.roll(row, shift, row.ndim - 1) if shift else row
                    total = row if total is None else jnp.where(lane // width == j, row, total)
                dst[e, g] = total

    has_left, has_right = my > 0, my < gy - 1

    def unpack(src, a, fields, own, count, width, last, rows):
        per = 128 // width
        lane = lanes_of((NZ, 128))
        for i in rows:
            dx = -1 if i < 0 else (1 if i >= count else 0)
            j = i - dx * count
            keep_r, keep_l = has_right, has_left
            if dx:
                keep_r, keep_l = keep_r & there(dx), keep_l & there(dx)
            from_r, from_l = src[0, 1 - dx, j // per], src[1, 1 - dx, j // per]
            shift = (128 - width * (j % per)) % 128
            from_r = pltpu.roll(from_r, shift, from_r.ndim - 1) if shift else from_r
            shift = (shift + 128 - width) % 128
            from_l = pltpu.roll(from_l, shift, from_l.ndim - 1) if shift else from_l
            row = jnp.where((lane < width) & keep_r, from_r, jnp.where((lane >= 128 - width) & keep_l, from_l, 0.0))
            a[fields, own + i, :, pl.ds(last, 128)] = row

    all_fields, coefs = slice(0, 5), slice(1, 5)
    sides = [(dx, dy) for dy in (1, -1) for dx in (0, -1, 1)]
    pack(l0.a, all_fields, 4, 32, 4, 128, send0)
    send([("y0", *p) for p in sides])

    l0.coarsen(0, 16, l1)
    pack(l1.a, coefs, 16, 16, 16, 0, send1)
    send([("x1", 1), ("x1", -1)] + [("y1", *p) for p in sides])
    l1.coarsen(0, 8, l2)
    l2.coarsen(0, 4, l3)
    l3.coarsen(0, 2, l4)
    lane = lanes_of((NZ, 128))
    send4[...] = jnp.where(lane < 64, l4.a[1:5, 12], pltpu.roll(l4.a[1:5, 13], 64, 2))
    send([("y4", 1), ("y4", -1)])

    arrive([("x0", 1), ("x0f", 1), ("x0", -1)] + [("y0", *p) for p in sides])
    unpack(recv0, l0.a, all_fields, 4, 32, 4, 256, range(-4, 35))
    l0.diagonal(-3, 35)
    l0.first(-3, 35, l0.va)
    l0.sweep(-2, 34, l0.va, l0.vb)
    l0.restrict_residual(0, 32, l0.vb, l1)
    send([("xr", 1), ("xr", -1)])
    pack(l1.a, 0, 16, 16, 16, 0, sendr)
    send([("yr", *p) for p in sides])

    def join(own, from_r, from_l, size):
        shape = own.shape
        at = lanes_of(shape) & 63
        keep_r = (at >= size) & (at < 48) & has_right
        keep_l = (at >= 48) & has_left
        from_r = pltpu.roll(from_r, size, len(shape) - 1)
        from_l = pltpu.roll(from_l, 128 - size, len(shape) - 1)
        return jnp.where(at < size, own, jnp.where(keep_r, from_r, jnp.where(keep_l, from_l, 0.0)))

    arrive([("y4", 1), ("y4", -1)])
    wide4[...] = join(send4[...], recv4[0], recv4[1], 16)
    send([("x4", dx) for dx in far])

    arrive([("x1", 1), ("x1", -1)] + [("y1", *p) for p in sides])
    unpack(recv1, l1.a, coefs, 16, 16, 16, 128, range(-15, 30))
    l1.diagonal(-14, 30)
    l1.coarsen(-7, 15, l2)
    l2.diagonal(-6, 14)
    l2.coarsen(-3, 7, l3, fx_low=-4)
    l3.diagonal(-3, 7)
    l3.coarsen(-1, 2, l4)
    l4.diagonal(0, 2)

    arrive([("xr", 1), ("xr", -1)] + [("yr", *p) for p in sides])
    unpack(recvr, l1.a, 0, 16, 16, 16, 128, range(-14, 30))
    l1.first(-14, 30, l1.va)
    l1.sweep(-13, 29, l1.va, l1.vb)
    l1.restrict_residual(-12, 28, l1.vb, l2)
    l2.first(-6, 14, l2.va)
    l2.sweep(-5, 13, l2.va, l2.vb)
    l2.restrict_residual(-4, 12, l2.vb, l3)
    l3.first(-2, 6, l3.va)
    l3.sweep(-1, 5, l3.va, l3.vb)
    l3.restrict_residual(0, 4, l3.vb, l4)
    l4.first(0, 2, l4.va)

    def two(ref, i):
        return jnp.where(lane < 64, ref[i], pltpu.roll(ref[i + 1], 64, 1))

    sendv[0] = two(l4.va, 12)
    for n in range(2):
        sendv[1 + n] = two(l3.a.at[0], 4 + 2 * n)
        sendv[3 + n] = two(l3.vb, 4 + 2 * n)
    send([("yv", 1), ("yv", -1)])

    def spread_two(both, ref, i):
        ref[i] = both
        ref[i + 1] = pltpu.roll(both, 64, both.ndim - 1)

    def own_and_far(ref, n_field, i_own):
        return

    arrive([("x4", dx) for dx in far])
    for n, dx in list(enumerate(far)) + [(None, 0)]:
        both = wide4[...] if dx == 0 else recv4x[n]
        i = 12 - 2 * dx
        l4.a[1:5, i] = both
        l4.a[1:5, i + 1] = pltpu.roll(both, 64, 2)
    l4.diagonal(-11, 13)
    l4.coarsen(-5, 6, l5, fx_low=-6)
    l5.diagonal(-5, 6)

    arrive([("yv", 1), ("yv", -1)])
    widev[0] = join(sendv[0], recvv[0, 0], recvv[1, 0], 16)
    send([("xv", dx) for dx in far])
    widev[1:5] = join(sendv[1:5], recvv[0, 1:5], recvv[1, 1:5], 32)
    send([("x3", 1), ("x3", -1)])
    arrive([("xv", dx) for dx in far])
    for n, dx in list(enumerate(far)) + [(None, 0)]:
        spread_two(widev[0] if dx == 0 else recvvx[n], l4.va, 12 - 2 * dx)

    def body(i, k):
        l4.a[0, pl.ds(i + 12, k)] = l4.rows(l4.va, i, k) * l4.rows(l4.d, i, k) * (1 / DAMPING)

    chunks(-11, 13, 8, body)
    l4.sweep(-11, 13, l4.va, l4.vb)
    l4.restrict_residual(-10, 12, l4.vb, l5)

    l5.first(-5, 6, l5.va)
    l5.sweep(-4, 5, l5.va, l5.vb)
    l5.sweep(-3, 4, l5.vb, l5.va)
    l5.sweep(-2, 3, l5.va, l5.vb)

    l4.correct(-4, 6, l4.vb, l5, l5.vb, l4.va)
    l4.sweep(-3, 5, l4.va, l4.vb)
    l4.sweep(-2, 4, l4.vb, l4.va)

    arrive([("x3", 1), ("x3", -1)])
    for src, dx in ((widev.at[pl.ds(1, 4)], 0), (recv3x.at[0], 1), (recv3x.at[1], -1)):
        for n in range(2):
            i = 4 - 4 * dx + 2 * n
            spread_two(src[n], l3.a.at[0], i)
            spread_two(src[2 + n], l3.vb, i)
    l3.correct(-4, 8, l3.vb, l4, l4.va, l3.va)
    l3.sweep(-3, 7, l3.va, l3.vb)
    l3.sweep(-2, 6, l3.vb, l3.va)

    l2.correct(-4, 12, l2.vb, l3, l3.va, l2.va)
    l2.sweep(-3, 11, l2.va, l2.vb)
    l2.sweep(-2, 10, l2.vb, l2.va)

    l1.correct(-4, 20, l1.vb, l2, l2.va, l1.va)
    l1.sweep(-2, 18, l1.va, l1.vb)
    l1.sweep(-1, 17, l1.vb, l1.va)

    l0.correct(-2, 34, l0.vb, l1, l1.va, l0.va)
    l0.sweep(-1, 33, l0.va, l0.vb)

    def last(n, c):
        for q in range(2):
            i = 8 * n + 4 * q
            mid, total = l0.beside(l0.vb, i, 4)
            new = (1 - DAMPING) * mid + l0.rows(l0.rd, i, 4) * (l0.field(0, i, 4) + total)
            for j in range(4):
                for h in range(2):
                    out_v.at[h].reshape(256, 128)[pl.ds(i + j, NZ, stride=32), :] = new[j, :, 128 * h : 128 * h + 128]
        return c

    for n in range(4):
        last(n, 0)
        for h in range(2):
            rows, cols = pl.ds(8 * n, 8), pl.ds(128 * h, 128)
            pltpu.make_async_copy(out_v.at[h, :, rows], field.at[:, rows, cols], store_sem.at[n, h]).start()

    grouped(list(transfers), lambda c: c.wait_send(), 1)
    for n in range(4):
        for h in range(2):
            rows, cols = pl.ds(8 * n, 8), pl.ds(128 * h, 128)
            pltpu.make_async_copy(out_v.at[h, :, rows], field.at[:, rows, cols], store_sem.at[n, h]).wait()


def solution(mesh):
    gx, gy = mesh.shape["gx"], mesh.shape["gy"]
    number = 2 + 1 + 2 + 2 + 18 + 4 + 4 * REACH + 2

    def step(*args):
        scratch = [
            pltpu.VMEM((2, NZ, R0, 128), F32),
            pltpu.VMEM((2, 4, NZ, R0, 128), jnp.bfloat16),
            pltpu.VMEM((2, 4, NZ * R0, 128), F32),
            pltpu.VMEM((2, NZ, R0, 128), F32),
        ]
        for rows, cols in zip(ROWS, LANES):
            scratch.append(pltpu.VMEM((5, rows, NZ, cols), F32))
            scratch += [pltpu.VMEM((rows, NZ, cols), F32)] * 4
        scratch += [
            pltpu.VMEM((2, 1, 5, NZ, 128), F32),
            pltpu.VMEM((2, 3, 1, 5, NZ, 128), F32),
            pltpu.VMEM((2, 2, 4, NZ, 128), F32),
            pltpu.VMEM((2, 3, 2, 4, NZ, 128), F32),
            pltpu.VMEM((2, 2, NZ, 128), F32),
            pltpu.VMEM((2, 3, 2, NZ, 128), F32),
            pltpu.VMEM((4, NZ, 128), F32),
            pltpu.VMEM((2, 4, NZ, 128), F32),
            pltpu.VMEM((4, NZ, 128), F32),
            pltpu.VMEM((2 * REACH, 4, NZ, 128), F32),
            pltpu.VMEM((5, NZ, 128), F32),
            pltpu.VMEM((2, 5, NZ, 128), F32),
            pltpu.VMEM((5, NZ, 128), F32),
            pltpu.VMEM((2 * REACH, NZ, 128), F32),
            pltpu.VMEM((2, 4, NZ, 128), F32),
            pltpu.SemaphoreType.DMA((2, 5)),
            pltpu.SemaphoreType.DMA((4, 2)),
            pltpu.SemaphoreType.DMA((number,)),
            pltpu.SemaphoreType.DMA((number,)),
        ]

        def body(*refs):
            kernel(gx, gy, *refs)

        return pl.pallas_call(
            body,
            out_shape=jax.ShapeDtypeStruct((NZ, R0, C0), F32),
            in_specs=[pl.BlockSpec(memory_space=pl.ANY)] * 5,
            out_specs=pl.BlockSpec(memory_space=pl.ANY),
            scratch_shapes=scratch,
            compiler_params=pltpu.CompilerParams(
                collective_id=0, has_side_effects=True, vmem_limit_bytes=40 * 2**20
            ),
        )(*args)

    placed = P(None, "gx", "gy")
    return jax.shard_map(step, mesh=mesh, in_specs=(placed,) * 5, out_specs=placed, check_vma=False)
```

```python
import jax
import jax.numpy as jnp
from jax import lax
from jax.experimental import pallas as pl
from jax.experimental.pallas import tpu as pltpu
from jax.sharding import PartitionSpec as P

DAMPING = 0.8
F32 = jnp.float32
MESH = pl.DeviceIdType.MESH
NZ, R0, C0 = 8, 32, 256
OWN = (4, 16, 8, 4, 12, 6)
ROWS = (40, 48, 24, 12, 26, 12)
LANES = (384, 256, 128, 128, 128, 128)
REACH = 6


def lanes_of(shape):
    return lax.broadcasted_iota(jnp.int32, shape, len(shape) - 1)


def left(values):
    return pltpu.roll(values, values.shape[-1] - 1, values.ndim - 1)


def right(values):
    return pltpu.roll(values, 1, values.ndim - 1)


def above(values):
    return pltpu.roll(values, values.shape[-2] - 1, values.ndim - 2)


def below(values):
    return pltpu.roll(values, 1, values.ndim - 2)


def take(values, index):
    rows = values.size // 128
    flat = jnp.take_along_axis(values.reshape(rows, 128), jnp.broadcast_to(index, (rows, 128)), axis=1)
    return flat.reshape(values.shape)


def squeeze(first, second, odd=False):
    lane = lanes_of((1, 128))
    index = (2 * lane + (1 if odd else 0)) & 127
    one = take(first, index)
    if second is None:
        return one
    return jnp.where(lanes_of(first.shape) < 64, one, take(second, index))


def pair(values):
    return values + pltpu.roll(values, 127, values.ndim - 1)


def squeeze_wide(values, odd=False, sums=True):
    parts = [values[..., 128 * j : 128 * j + 128] for j in range(values.shape[-1] // 128)]
    if sums:
        parts = [pair(p) for p in parts]
    return squeeze(parts[0], parts[1] if len(parts) > 1 else None, odd)


def stretch_index(kind):
    lane = lanes_of((1, 128))
    half = lane // 2
    if kind == "low":
        return half
    if kind == "high":
        return half + 64
    split = 64 if kind == "ends" else 96
    return half + jnp.where(lane >= split, 64, 0)


def chunks(lo, hi, step, body):
    for i in range(lo, hi, step):
        body(i, min(step, hi - i))


class Level:
    def __init__(self, level, a, d, rd, va, vb):
        self.level, self.a, self.d, self.rd, self.va, self.vb = level, a, d, rd, va, vb
        self.own = OWN[level]
        self.step = (38, 44, 24, 12, 26, 12)[level]

    def rows(self, ref, i, k):
        return ref[pl.ds(i + self.own, k)]

    def field(self, f, i, k):
        return self.a[f, pl.ds(i + self.own, k)]

    def diagonal(self, lo, hi):
        def body(i, k):
            kappa = self.field(1, i, k)
            fx, fxl, fy, fz = self.field(2, i, k), self.field(2, i - 1, k), self.field(3, i, k), self.field(4, i, k)
            d = kappa + fx + fxl + fy + right(fy) + fz + below(fz)
            self.d[pl.ds(i + self.own, k)] = d
            self.rd[pl.ds(i + self.own, k)] = jnp.where(kappa > 0, DAMPING / d, 0.0)

        chunks(lo, hi, self.step, body)

    def beside(self, v, i, k):
        c = self.rows(v, i, k)
        fx, fxl, fy, fz = self.field(2, i, k), self.field(2, i - 1, k), self.field(3, i, k), self.field(4, i, k)
        total = fx * self.rows(v, i + 1, k) + fxl * self.rows(v, i - 1, k)
        total = total + fy * left(c) + right(fy * c)
        total = total + fz * above(c) + below(fz * c)
        return c, total

    def first(self, lo, hi, out):
        def body(i, k):
            out[pl.ds(i + self.own, k)] = self.rows(self.rd, i, k) * self.field(0, i, k)

        chunks(lo, hi, self.step, body)

    def sweep(self, lo, hi, v, out):
        def body(i, k):
            c, total = self.beside(v, i, k)
            new = (1 - DAMPING) * c + self.rows(self.rd, i, k) * (self.field(0, i, k) + total)
            out[pl.ds(i + self.own, k)] = new

        chunks(lo, hi, self.step, body)

    def restrict_residual(self, lo, hi, v, coarse):
        def body(n, m):
            k = 2 * m
            i = 2 * n
            c, total = self.beside(v, i, k)
            residual = self.field(0, i, k) - self.rows(self.d, i, k) * c + total
            residual = residual[..., : min(residual.shape[-1], 256)]
            residual = residual.reshape(m, 2, *residual.shape[1:])
            coarse.a[0, pl.ds(n + coarse.own, m)] = fit(squeeze_wide(residual[:, 0] + residual[:, 1]) * 0.25, coarse)

        chunks(lo // 2, hi // 2, self.step // 2, body)

    def coarsen(self, lo, hi, coarse, fx_low=None):
        def body(n, m):
            both = [self.field(f, 2 * n, 2 * m)[..., : min(self.a.shape[-1], 256)] for f in (1, 2, 3, 4)]
            both = [b.reshape(m, 2, *b.shape[1:]) for b in both]
            kappa, fx, fy, fz = both
            at = pl.ds(n + coarse.own, m)
            coarse.a[1, at] = fit(squeeze_wide(kappa[:, 0] + kappa[:, 1]) * 0.25, coarse)
            coarse.a[2, at] = fit(squeeze_wide(fx[:, 1]) * 0.25, coarse)
            coarse.a[3, at] = fit(squeeze_wide(fy[:, 0] + fy[:, 1], odd=True, sums=False) * 0.25, coarse)
            coarse.a[4, at] = fit(squeeze_wide(fz[:, 0] + fz[:, 1]) * 0.25, coarse)

        chunks(lo, hi, self.step // 2, body)
        if fx_low is not None:
            fx = self.field(2, 2 * fx_low + 1, 1)
            coarse.a[2, pl.ds(fx_low + coarse.own, 1)] = squeeze_wide(fx) * 0.25

    def correct(self, lo, hi, v, coarse, c, out):
        def body(n, m):
            values = c[pl.ds(n + coarse.own, m)]
            if self.level == 0:
                first, second = values[..., :128], values[..., 128:]
                fine = [take(first, stretch_index("low")), take(first, stretch_index("high")), take(second, stretch_index("ends"))]
            elif self.level == 1:
                fine = [take(values, stretch_index("low")), take(values, stretch_index("high"))]
            else:
                fine = [take(values, stretch_index("late"))]
            for j, part in enumerate(fine):
                cols = slice(128 * j, 128 * j + 128)
                at = pl.ds(2 * n + self.own, 2 * m)
                spread = jnp.broadcast_to(part[:, None], (m, 2, NZ, 128)).reshape(2 * m, NZ, 128)
                out[at, :, cols] = v[at, :, cols] + spread

        chunks(lo // 2, hi // 2, max(self.step // 2, 1), body)


def fit(values, coarse):
    if coarse.level == 1:
        return jnp.concatenate([values, jnp.zeros_like(values)], axis=-1)
    return values


def kernel(gx, gy, source, kappa_sq, face_x, face_y, face_z, field, *refs):
    refs = list(refs)

    def get(n):
        out = refs[:n]
        del refs[:n]
        return out

    raw_s, raw_c, wide, out_v = get(4)
    levels = []
    for n in range(6):
        levels.append(Level(n, *get(5)))
    send0, recv0, send1, recv1, sendr, recvr = get(6)
    pack4, side4 = get(2)
    sendv, recvv, widev, recvvx, recv3x = get(5)
    load_sem, store_sem, ssem, rsem, known = get(5)
    l0, l1, l2, l3, l4, l5 = levels

    mx, my = lax.axis_index("gx"), lax.axis_index("gy")

    def there(dx):
        if dx == 0:
            return None
        return mx + dx < gx if dx > 0 else mx + dx >= 0

    def when(cond, action):
        if cond is None:
            action()
        else:
            pl.when(cond)(action)

    far = [s * k for k in range(1, REACH + 1) for s in (1, -1)]

    barrier = pltpu.get_barrier_semaphore()
    partners = [(dx, dy) for dx in (0, 1, -1) for dy in (0, 1, -1) if dx or dy]
    count = 0
    for dx in (0, 1, -1):
        group = [p for p in partners if p[0] == dx]

        def greet(group=group):
            for px, py in group:
                ids = (mx + px, lax.rem(my + py + gy, gy))
                pl.semaphore_signal(barrier, inc=1, device_id=ids, device_id_type=MESH)

        when(there(dx), greet)
        count = count + (len(group) if dx == 0 else jnp.where(there(dx), len(group), 0))

    loads = []
    for h in range(2):
        cols = pl.ds(128 * h, 128)
        loads.append(pltpu.make_async_copy(source.at[:, :, cols], raw_s.at[h], load_sem.at[h, 0]))
        for f, ref in enumerate((kappa_sq, face_x, face_y, face_z)):
            loads.append(pltpu.make_async_copy(ref.at[:, :, cols], raw_c.at[h, f], load_sem.at[h, f + 1]))
    for copy in loads:
        copy.start()

    transfers = {}

    def plan(name, src, dst, dx, dy):
        transfers[name] = (src, dst, dx, dy, len(transfers))

    def copy_of(name):
        src, dst, dx, dy, n = transfers[name]
        ids = (mx + dx, lax.rem(my + dy + gy, gy))
        return pltpu.make_async_remote_copy(
            src_ref=src, dst_ref=dst, send_sem=ssem.at[n], recv_sem=rsem.at[n], device_id=ids, device_id_type=MESH
        )

    def grouped(names, action, sign):
        by = {}
        for name in names:
            by.setdefault(transfers[name][2], []).append(name)
        for dx, group in by.items():

            def go(group=group):
                for name in group:
                    action(copy_of(name))

            when(there(sign * dx), go)

    def send(names):
        grouped(names, lambda c: c.start(), 1)

    def arrive(names):
        grouped(names, lambda c: c.wait_recv(), -1)

    for d in (1, -1):
        a0, a1 = l0.a, l1.a
        s0, t0 = (33, 1) if d == 1 else (4, 36)
        cols = pl.ds(0, C0)
        plan(("x0", d), a0.at[:, pl.ds(s0, 3), :, cols], a0.at[:, pl.ds(t0, 3), :, cols], d, 0)
        if d == 1:
            plan(("x0f", d), a0.at[2, pl.ds(32, 1), :, cols], a0.at[2, pl.ds(0, 1), :, cols], d, 0)
        cols = pl.ds(0, 128)
        s1, t1, n1 = (17, 1, 15) if d == 1 else (16, 32, 14)
        plan(("x1", d), a1.at[pl.ds(1, 4), pl.ds(s1, n1), :, cols], a1.at[pl.ds(1, 4), pl.ds(t1, n1), :, cols], d, 0)
        s1, t1 = (18, 2) if d == 1 else (16, 32)
        plan(("xr", d), a1.at[0, pl.ds(s1, 14), :, cols], a1.at[0, pl.ds(t1, 14), :, cols], d, 0)
    for dy in (1, -1):
        e = (dy + 1) // 2
        for dx in (-1, 0, 1):
            plan(("y0", dx, dy), send0.at[e], recv0.at[e, dx + 1], dx, dy)
            plan(("y1", dx, dy), send1.at[e], recv1.at[e, dx + 1], dx, dy)
            plan(("yr", dx, dy), sendr.at[e], recvr.at[e, dx + 1], dx, dy)
        plan(("y4", dy), pack4, side4.at[e], 0, dy)
        plan(("yv", dy), sendv, recvv.at[e], 0, dy)
    for n, dx in enumerate(far):
        plan(("x4", dx), pack4.at[2 * REACH], pack4.at[n], dx, 0)
        plan(("xv", dx), widev.at[0], recvvx.at[n], dx, 0)
    for n, dx in enumerate((1, -1)):
        plan(("x3", dx), widev.at[pl.ds(1, 4)], recv3x.at[n], dx, 0)

    def tell(word):
        for e, dx in enumerate((2, -2)):

            def go(e=e, dx=dx):
                pl.semaphore_signal(known.at[word, e], inc=1, device_id=(mx + dx, my), device_id_type=MESH)

            when(there(dx), go)

    def hear(word):
        for e, dx in enumerate((2, -2)):
            when(there(-dx), lambda e=e: pl.semaphore_wait(known.at[word, e], 1))

    def zero(ref, *index):
        ref[index] = jnp.zeros(ref[index].shape, F32)

    @pl.when(mx == 0)
    def _():
        l0.a[:, 0:4] = jnp.zeros((5, 4, NZ, 384), F32)
        l1.a[:, 0:16] = jnp.zeros((5, 16, NZ, 256), F32)
        recv3x[0] = jnp.zeros((4, NZ, 128), F32)

    @pl.when(mx == gx - 1)
    def _():
        l0.a[:, 36:40] = jnp.zeros((5, 4, NZ, 384), F32)
        l1.a[:, 32:48] = jnp.zeros((5, 16, NZ, 256), F32)
        recv3x[1] = jnp.zeros((4, NZ, 128), F32)

    for n, dx in enumerate(far):

        @pl.when(jnp.logical_not(there(-dx)))
        def _(n=n):
            pack4[n] = jnp.zeros((NZ, 128), F32)
            recvvx[n] = jnp.zeros((NZ, 128), F32)

    for copy in loads:
        copy.wait()

    def widen(h, c):
        for f in range(4):
            wide[h, f] = raw_c[h, f].reshape(256, 128).astype(F32)
        top = pl.ds(224, 32)
        wide[h, 0, top] = wide[h, 0, top] + wide[h, 3, top]
        wide[h, 3, top] = jnp.zeros((32, 128), F32)
        return c

    for h in range(2):
        widen(h, 0)

    def turn(i):
        for h in range(2):
            cols = slice(128 * h, 128 * h + 128)
            l0.a[0, 4 + i, :, cols] = raw_s.at[h].reshape(256, 128)[pl.ds(i, NZ, stride=32), :]
            for f in range(4):
                l0.a[1 + f, 4 + i, :, cols] = wide.at[h, f][pl.ds(i, NZ, stride=32), :]

    edge = [0, 1, 2, 28, 29, 30, 31]
    for i in edge:
        turn(i)
    pl.semaphore_wait(barrier, count)
    send([("x0", 1), ("x0f", 1), ("x0", -1)])
    for i in range(3, 28):
        turn(i)

    def pack(a, fields, own, count, width, last, dst):
        per = 128 // width
        lane = lanes_of((NZ, 128))
        for e in range(2):
            at = pl.ds(last, 128) if e == 1 else pl.ds(0, 128)
            for g in range(count // per):
                total = None
                for j in range(per):
                    row = a[fields, own + g * per + j, :, at]
                    shift = (width * j + (width if e == 1 else 0)) % 128
                    row = pltpu.roll(row, shift, row.ndim - 1) if shift else row
                    total = row if total is None else jnp.where(lane // width == j, row, total)
                dst[e, g] = total

    has_left, has_right = my > 0, my < gy - 1

    def unpack(src, a, fields, own, count, width, last, rows):
        per = 128 // width
        lane = lanes_of((NZ, 128))
        for i in rows:
            dx = -1 if i < 0 else (1 if i >= count else 0)
            j = i - dx * count
            keep_r, keep_l = has_right, has_left
            if dx:
                keep_r, keep_l = keep_r & there(dx), keep_l & there(dx)
            from_r, from_l = src[0, 1 - dx, j // per], src[1, 1 - dx, j // per]
            shift = (128 - width * (j % per)) % 128
            from_r = pltpu.roll(from_r, shift, from_r.ndim - 1) if shift else from_r
            shift = (shift + 128 - width) % 128
            from_l = pltpu.roll(from_l, shift, from_l.ndim - 1) if shift else from_l
            row = jnp.where((lane < width) & keep_r, from_r, jnp.where((lane >= 128 - width) & keep_l, from_l, 0.0))
            a[fields, own + i, :, pl.ds(last, 128)] = row

    all_fields, coefs = slice(0, 5), slice(1, 5)
    sides = [(dx, dy) for dy in (1, -1) for dx in (0, -1, 1)]
    pack(l0.a, all_fields, 4, 32, 4, 128, send0)
    send([("y0", *p) for p in sides])

    l0.coarsen(0, 16, l1)
    pack(l1.a, coefs, 16, 16, 16, 0, send1)
    send([("x1", 1), ("x1", -1)] + [("y1", *p) for p in sides])
    l1.coarsen(0, 8, l2)
    l2.coarsen(0, 4, l3)
    l3.coarsen(0, 2, l4)
    lane = lanes_of((NZ, 128))
    total = l4.a[1, 12]
    for q in range(1, 8):
        total = jnp.where(lane < 16 * q, total, pltpu.roll(l4.a[1 + q // 2, 12 + q % 2], 16 * q, 1))
    pack4[2 * REACH] = total

    arrive([("x0", 1), ("x0f", 1), ("x0", -1)] + [("y0", *p) for p in sides])
    tell(0)
    unpack(recv0, l0.a, all_fields, 4, 32, 4, 256, range(-4, 35))
    l0.diagonal(-3, 35)
    l0.first(-3, 35, l0.va)
    l0.sweep(-2, 34, l0.va, l0.vb)
    l0.restrict_residual(0, 32, l0.vb, l1)
    send([("xr", 1), ("xr", -1)])
    pack(l1.a, 0, 16, 16, 16, 0, sendr)
    send([("yr", *p) for p in sides])

    def join(own, from_r, from_l, size):
        shape = own.shape
        at = lanes_of(shape) & 63
        keep_r = (at >= size) & (at < 48) & has_right
        keep_l = (at >= 48) & has_left
        from_r = pltpu.roll(from_r, size, len(shape) - 1)
        from_l = pltpu.roll(from_l, 128 - size, len(shape) - 1)
        return jnp.where(at < size, own, jnp.where(keep_r, from_r, jnp.where(keep_l, from_l, 0.0)))


    arrive([("x1", 1), ("x1", -1)] + [("y1", *p) for p in sides])
    unpack(recv1, l1.a, coefs, 16, 16, 16, 128, range(-15, 30))
    hear(0)
    tell(1)
    l1.diagonal(-14, 30)
    l1.coarsen(-7, 15, l2)
    l2.diagonal(-6, 14)
    l2.coarsen(-3, 7, l3, fx_low=-4)
    l3.diagonal(-3, 7)
    l3.coarsen(-1, 2, l4)
    l4.diagonal(0, 2)

    arrive([("xr", 1), ("xr", -1)] + [("yr", *p) for p in sides])
    unpack(recvr, l1.a, 0, 16, 16, 16, 128, range(-14, 30))
    l1.first(-14, 30, l1.va)
    l1.sweep(-13, 29, l1.va, l1.vb)
    l1.restrict_residual(-12, 28, l1.vb, l2)
    hear(1)
    send([("x4", dx) for dx in far])
    l2.first(-6, 14, l2.va)
    l2.sweep(-5, 13, l2.va, l2.vb)
    l2.restrict_residual(-4, 12, l2.vb, l3)
    l3.first(-2, 6, l3.va)
    l3.sweep(-1, 5, l3.va, l3.vb)
    l3.restrict_residual(0, 4, l3.vb, l4)
    l4.first(0, 2, l4.va)

    def two(ref, i):
        return jnp.where(lane < 64, ref[i], pltpu.roll(ref[i + 1], 64, 1))

    sendv[0] = two(l4.va, 12)
    for n in range(2):
        sendv[1 + n] = two(l3.a.at[0], 4 + 2 * n)
        sendv[3 + n] = two(l3.vb, 4 + 2 * n)
    send([("yv", 1), ("yv", -1)])

    def spread_two(both, ref, i):
        ref[i] = both
        ref[i + 1] = pltpu.roll(both, 64, both.ndim - 1)

    arrive([("yv", 1), ("yv", -1)])
    widev[0] = join(sendv[0], recvv[0, 0], recvv[1, 0], 16)
    send([("xv", dx) for dx in far])
    widev[1:5] = join(sendv[1:5], recvv[0, 1:5], recvv[1, 1:5], 32)
    send([("x3", 1), ("x3", -1)])

    arrive([("x4", dx) for dx in far])
    send([("y4", 1), ("y4", -1)])
    arrive([("y4", 1), ("y4", -1)])
    keep_r, keep_l = (lane < 64) & has_right, (lane >= 64) & has_left
    for n, dx in enumerate(far + [0]):
        i = 12 - 2 * dx
        own, from_r, from_l = pack4[n], side4[0, n], side4[1, n]
        for q in range(8):
            parts = [pltpu.roll(p, b % 128, 1) if b % 128 else p for p, b in ((own, -16 * q), (from_r, 16 - 16 * q), (from_l, -16 - 16 * q))]
            row = jnp.where(lane < 16, parts[0], jnp.where(keep_r, parts[1], jnp.where(keep_l, parts[2], 0.0)))
            l4.a[1 + q // 2, i + q % 2] = row
    l4.diagonal(-11, 13)
    l4.coarsen(-5, 6, l5, fx_low=-6)
    l5.diagonal(-5, 6)

    arrive([("xv", dx) for dx in far])
    for n, dx in list(enumerate(far)) + [(None, 0)]:
        spread_two(widev[0] if dx == 0 else recvvx[n], l4.va, 12 - 2 * dx)

    def body(i, k):
        l4.a[0, pl.ds(i + 12, k)] = l4.rows(l4.va, i, k) * l4.rows(l4.d, i, k) * (1 / DAMPING)

    chunks(-11, 13, 8, body)
    l4.sweep(-11, 13, l4.va, l4.vb)
    l4.restrict_residual(-10, 12, l4.vb, l5)

    l5.first(-5, 6, l5.va)
    l5.sweep(-4, 5, l5.va, l5.vb)
    l5.sweep(-3, 4, l5.vb, l5.va)
    l5.sweep(-2, 3, l5.va, l5.vb)

    l4.correct(-4, 6, l4.vb, l5, l5.vb, l4.va)
    l4.sweep(-3, 5, l4.va, l4.vb)
    l4.sweep(-2, 4, l4.vb, l4.va)

    arrive([("x3", 1), ("x3", -1)])
    for src, dx in ((widev.at[pl.ds(1, 4)], 0), (recv3x.at[0], 1), (recv3x.at[1], -1)):
        for n in range(2):
            i = 4 - 4 * dx + 2 * n
            spread_two(src[n], l3.a.at[0], i)
            spread_two(src[2 + n], l3.vb, i)
    l3.correct(-4, 8, l3.vb, l4, l4.va, l3.va)
    l3.sweep(-3, 7, l3.va, l3.vb)
    l3.sweep(-2, 6, l3.vb, l3.va)

    l2.correct(-4, 12, l2.vb, l3, l3.va, l2.va)
    l2.sweep(-3, 11, l2.va, l2.vb)
    l2.sweep(-2, 10, l2.vb, l2.va)

    l1.correct(-4, 20, l1.vb, l2, l2.va, l1.va)
    l1.sweep(-2, 18, l1.va, l1.vb)
    l1.sweep(-1, 17, l1.vb, l1.va)

    l0.correct(-2, 34, l0.vb, l1, l1.va, l0.va)
    l0.sweep(-1, 33, l0.va, l0.vb)

    def last(n, c):
        for q in range(2):
            i = 8 * n + 4 * q
            mid, total = l0.beside(l0.vb, i, 4)
            new = (1 - DAMPING) * mid + l0.rows(l0.rd, i, 4) * (l0.field(0, i, 4) + total)
            for j in range(4):
                for h in range(2):
                    out_v.at[h].reshape(256, 128)[pl.ds(i + j, NZ, stride=32), :] = new[j, :, 128 * h : 128 * h + 128]
        return c

    for n in range(4):
        last(n, 0)
        for h in range(2):
            rows, cols = pl.ds(8 * n, 8), pl.ds(128 * h, 128)
            pltpu.make_async_copy(out_v.at[h, :, rows], field.at[:, rows, cols], store_sem.at[n, h]).start()

    grouped(list(transfers), lambda c: c.wait_send(), 1)
    for n in range(4):
        for h in range(2):
            rows, cols = pl.ds(8 * n, 8), pl.ds(128 * h, 128)
            pltpu.make_async_copy(out_v.at[h, :, rows], field.at[:, rows, cols], store_sem.at[n, h]).wait()


def solution(mesh):
    gx, gy = mesh.shape["gx"], mesh.shape["gy"]
    number = 2 + 1 + 2 + 2 + 18 + 4 + 4 * REACH + 2

    def step(*args):
        scratch = [
            pltpu.VMEM((2, NZ, R0, 128), F32),
            pltpu.VMEM((2, 4, NZ, R0, 128), jnp.bfloat16),
            pltpu.VMEM((2, 4, NZ * R0, 128), F32),
            pltpu.VMEM((2, NZ, R0, 128), F32),
        ]
        for rows, cols in zip(ROWS, LANES):
            scratch.append(pltpu.VMEM((5, rows, NZ, cols), F32))
            scratch += [pltpu.VMEM((rows, NZ, cols), F32)] * 4
        scratch += [
            pltpu.VMEM((2, 1, 5, NZ, 128), F32),
            pltpu.VMEM((2, 3, 1, 5, NZ, 128), F32),
            pltpu.VMEM((2, 2, 4, NZ, 128), F32),
            pltpu.VMEM((2, 3, 2, 4, NZ, 128), F32),
            pltpu.VMEM((2, 2, NZ, 128), F32),
            pltpu.VMEM((2, 3, 2, NZ, 128), F32),
            pltpu.VMEM((2 * REACH + 1, NZ, 128), F32),
            pltpu.VMEM((2, 2 * REACH + 1, NZ, 128), F32),
            pltpu.VMEM((5, NZ, 128), F32),
            pltpu.VMEM((2, 5, NZ, 128), F32),
            pltpu.VMEM((5, NZ, 128), F32),
            pltpu.VMEM((2 * REACH, NZ, 128), F32),
            pltpu.VMEM((2, 4, NZ, 128), F32),
            pltpu.SemaphoreType.DMA((2, 5)),
            pltpu.SemaphoreType.DMA((4, 2)),
            pltpu.SemaphoreType.DMA((number,)),
            pltpu.SemaphoreType.DMA((number,)),
            pltpu.SemaphoreType.REGULAR((2, 2)),
        ]

        def body(*refs):
            kernel(gx, gy, *refs)

        return pl.pallas_call(
            body,
            out_shape=jax.ShapeDtypeStruct((NZ, R0, C0), F32),
            in_specs=[pl.BlockSpec(memory_space=pl.ANY)] * 5,
            out_specs=pl.BlockSpec(memory_space=pl.ANY),
            scratch_shapes=scratch,
            compiler_params=pltpu.CompilerParams(
                collective_id=0, has_side_effects=True, vmem_limit_bytes=60 * 2**20
            ),
        )(*args)

    placed = P(None, "gx", "gy")
    return jax.shard_map(step, mesh=mesh, in_specs=(placed,) * 5, out_specs=placed, check_vma=False)
```

```python
import jax
import jax.numpy as jnp
from jax import lax
from jax.experimental import pallas as pl
from jax.experimental.pallas import tpu as pltpu
from jax.sharding import PartitionSpec as P

DAMPING = 0.8
F32 = jnp.float32
MESH = pl.DeviceIdType.MESH
NZ, R0, C0 = 8, 32, 256
OWN = (4, 8, 8, 4, 12, 6)
ROWS = (40, 32, 24, 12, 26, 12)
LANES = (384, 256, 128, 128, 128, 128)
REACH = 6
NSEM = 96
AROUND = [(dx, dy) for dx in (0, 1, -1) for dy in (0, 1, -1) if dx or dy]


def lanes_of(shape):
    return lax.broadcasted_iota(jnp.int32, shape, len(shape) - 1)


def left(values):
    return pltpu.roll(values, values.shape[-1] - 1, values.ndim - 1)


def right(values):
    return pltpu.roll(values, 1, values.ndim - 1)


def above(values):
    return pltpu.roll(values, values.shape[-2] - 1, values.ndim - 2)


def below(values):
    return pltpu.roll(values, 1, values.ndim - 2)


def take(values, index):
    rows = values.size // 128
    flat = jnp.take_along_axis(values.reshape(rows, 128), jnp.broadcast_to(index, (rows, 128)), axis=1)
    return flat.reshape(values.shape)


def squeeze(first, second, odd=False):
    lane = lanes_of((1, 128))
    index = (2 * lane + (1 if odd else 0)) & 127
    one = take(first, index)
    if second is None:
        return one
    return jnp.where(lanes_of(first.shape) < 64, one, take(second, index))


def pair(values):
    return values + pltpu.roll(values, 127, values.ndim - 1)


def squeeze_wide(values, odd=False, sums=True):
    parts = [values[..., 128 * j : 128 * j + 128] for j in range(values.shape[-1] // 128)]
    if sums:
        parts = [pair(p) for p in parts]
    return squeeze(parts[0], parts[1] if len(parts) > 1 else None, odd)


def stretch_index(kind):
    lane = lanes_of((1, 128))
    half = lane // 2
    if kind == "low":
        return half
    if kind == "high":
        return half + 64
    split = 64 if kind == "ends" else 96
    return half + jnp.where(lane >= split, 64, 0)


def chunks(lo, hi, step, body):
    for i in range(lo, hi, step):
        body(i, min(step, hi - i))


class Level:
    def __init__(self, level, a, d, rd, va, vb):
        self.level, self.a, self.d, self.rd, self.va, self.vb = level, a, d, rd, va, vb
        self.own = OWN[level]
        self.step = (38, 32, 24, 12, 26, 12)[level]

    def rows(self, ref, i, k):
        return ref[pl.ds(i + self.own, k)]

    def field(self, f, i, k):
        return self.a[f, pl.ds(i + self.own, k)]

    def diagonal(self, lo, hi):
        def body(i, k):
            kappa = self.field(1, i, k)
            fx, fxl, fy, fz = self.field(2, i, k), self.field(2, i - 1, k), self.field(3, i, k), self.field(4, i, k)
            d = kappa + fx + fxl + fy + right(fy) + fz + below(fz)
            self.d[pl.ds(i + self.own, k)] = d
            self.rd[pl.ds(i + self.own, k)] = jnp.where(kappa > 0, DAMPING / d, 0.0)

        chunks(lo, hi, self.step, body)

    def beside(self, v, i, k):
        c = self.rows(v, i, k)
        fx, fxl, fy, fz = self.field(2, i, k), self.field(2, i - 1, k), self.field(3, i, k), self.field(4, i, k)
        along_x = fx * self.rows(v, i + 1, k) + fxl * self.rows(v, i - 1, k)
        along_y = fy * left(c) + right(fy * c)
        along_z = fz * above(c) + below(fz * c)
        return c, (self.field(0, i, k) + along_x) + (along_y + along_z)

    def first(self, lo, hi, out):
        def body(i, k):
            out[pl.ds(i + self.own, k)] = self.rows(self.rd, i, k) * self.field(0, i, k)

        chunks(lo, hi, self.step, body)

    def sweep(self, lo, hi, v, out):
        def body(i, k):
            c, total = self.beside(v, i, k)
            new = (1 - DAMPING) * c + self.rows(self.rd, i, k) * total
            out[pl.ds(i + self.own, k)] = new

        chunks(lo, hi, self.step, body)

    def restrict_residual(self, lo, hi, v, coarse):
        def body(n, m):
            k = 2 * m
            i = 2 * n
            c, total = self.beside(v, i, k)
            residual = total - self.rows(self.d, i, k) * c
            residual = residual[..., : min(residual.shape[-1], 256)]
            residual = residual.reshape(m, 2, *residual.shape[1:])
            coarse.a[0, pl.ds(n + coarse.own, m)] = fit(squeeze_wide(residual[:, 0] + residual[:, 1]) * 0.25, coarse)

        chunks(lo // 2, hi // 2, self.step // 2, body)

    def coarsen(self, lo, hi, coarse, fx_low=None):
        def body(n, m):
            both = [self.field(f, 2 * n, 2 * m)[..., : min(self.a.shape[-1], 256)] for f in (1, 2, 3, 4)]
            both = [b.reshape(m, 2, *b.shape[1:]) for b in both]
            kappa, fx, fy, fz = both
            at = pl.ds(n + coarse.own, m)
            coarse.a[1, at] = fit(squeeze_wide(kappa[:, 0] + kappa[:, 1]) * 0.25, coarse)
            coarse.a[2, at] = fit(squeeze_wide(fx[:, 1]) * 0.25, coarse)
            coarse.a[3, at] = fit(squeeze_wide(fy[:, 0] + fy[:, 1], odd=True, sums=False) * 0.25, coarse)
            coarse.a[4, at] = fit(squeeze_wide(fz[:, 0] + fz[:, 1]) * 0.25, coarse)

        chunks(lo, hi, self.step // 2, body)
        if fx_low is not None:
            fx = self.field(2, 2 * fx_low + 1, 1)
            coarse.a[2, pl.ds(fx_low + coarse.own, 1)] = squeeze_wide(fx) * 0.25

    def correct(self, lo, hi, v, coarse, c, out):
        def body(n, m):
            values = c[pl.ds(n + coarse.own, m)]
            if self.level == 0:
                first, second = values[..., :128], values[..., 128:]
                fine = [take(first, stretch_index("low")), take(first, stretch_index("high")), take(second, stretch_index("ends"))]
            elif self.level == 1:
                fine = [take(values, stretch_index("low")), take(values, stretch_index("high"))]
            else:
                fine = [take(values, stretch_index("late"))]
            for j, part in enumerate(fine):
                cols = slice(128 * j, 128 * j + 128)
                at = pl.ds(2 * n + self.own, 2 * m)
                spread = jnp.broadcast_to(part[:, None], (m, 2, NZ, 128)).reshape(2 * m, NZ, 128)
                out[at, :, cols] = v[at, :, cols] + spread

        chunks(lo // 2, hi // 2, max(self.step // 2, 1), body)


def fit(values, coarse):
    if coarse.level == 1:
        return jnp.concatenate([values, jnp.zeros_like(values)], axis=-1)
    return values


def kernel(gx, gy, source, kappa_sq, face_x, face_y, face_z, field, *refs):
    refs = list(refs)

    def get(n):
        out = refs[:n]
        del refs[:n]
        return out

    raw_s, raw_c, wide, out_v = get(4)
    levels = []
    for n in range(6):
        levels.append(Level(n, *get(5)))
    send0, recv0, corner, recvc, send1, recv1, sendr, recvr = get(8)
    send3, recv3, sendk, recvk, send2, recv2 = get(6)
    pack4, side4, widev, recvvx, recv3x = get(5)
    load_sem, store_sem, ssem, rsem, known = get(5)
    l0, l1, l2, l3, l4, l5 = levels

    mx, my = lax.axis_index("gx"), lax.axis_index("gy")

    def there(dx):
        if dx == 0:
            return None
        return mx + dx < gx if dx > 0 else mx + dx >= 0

    def when(cond, action):
        if cond is None:
            action()
        else:
            pl.when(cond)(action)

    far = [s * k for k in range(REACH, 0, -1) for s in (1, -1)]

    barrier = pltpu.get_barrier_semaphore()
    partners = AROUND
    count = 0
    for dx in (0, 1, -1):
        group = [p for p in partners if p[0] == dx]

        def greet(group=group):
            for px, py in group:
                ids = (mx + px, lax.rem(my + py + gy, gy))
                pl.semaphore_signal(barrier, inc=1, device_id=ids, device_id_type=MESH)

        when(there(dx), greet)
        count = count + (len(group) if dx == 0 else jnp.where(there(dx), len(group), 0))

    loads = []
    for h in range(2):
        cols = pl.ds(128 * h, 128)
        loads.append(pltpu.make_async_copy(source.at[:, :, cols], raw_s.at[h], load_sem.at[h, 0]))
        for f, ref in enumerate((kappa_sq, face_x, face_y, face_z)):
            loads.append(pltpu.make_async_copy(ref.at[:, :, cols], raw_c.at[h, f], load_sem.at[h, f + 1]))
    for copy in loads:
        copy.start()

    transfers = {}

    def plan(name, src, dst, dx, dy):
        transfers[name] = (src, dst, dx, dy, len(transfers))

    def copy_of(name):
        src, dst, dx, dy, n = transfers[name]
        ids = (mx + dx, lax.rem(my + dy + gy, gy))
        return pltpu.make_async_remote_copy(
            src_ref=src, dst_ref=dst, send_sem=ssem.at[n], recv_sem=rsem.at[n], device_id=ids, device_id_type=MESH
        )

    def grouped(names, action, sign):
        by = {}
        for name in names:
            by.setdefault(transfers[name][2], []).append(name)
        reach = max(abs(dx) for dx in by)

        def group(dx):
            for name in by[dx]:
                action(copy_of(name))

        def every():
            for dx in by:
                group(dx)

        def some():
            for dx in by:
                when(there(sign * dx), lambda dx=dx: group(dx))

        if reach == 0:
            every()
        else:
            inside = (mx >= reach) & (mx < gx - reach)
            pl.when(inside)(every)
            pl.when(jnp.logical_not(inside))(some)

    def send(names):
        grouped(names, lambda c: c.start(), 1)

    def arrive(names):
        grouped(names, lambda c: c.wait_recv(), -1)

    a0, a1 = l0.a, l1.a
    cols, cols1 = pl.ds(0, C0), pl.ds(0, 128)

    def rows0(name, fields, src, dst, rows, d):
        plan((name, d), a0.at[fields, pl.ds(src, rows), :, cols], a0.at[fields, pl.ds(dst, rows), :, cols], d, 0)

    rows0("x0", pl.ds(0, 5), 34, 2, 2, 1)
    rows0("x0f", 2, 33, 1, 1, 1)
    rows0("x0", pl.ds(0, 5), 4, 36, 2, -1)
    rows0("x0b", pl.ds(0, 2), 33, 1, 1, 1)
    rows0("x0c", pl.ds(3, 2), 33, 1, 1, 1)
    rows0("x0d", 2, 32, 0, 1, 1)
    rows0("x0b", pl.ds(0, 5), 6, 38, 1, -1)
    for d, src, dst, n1, nr in ((1, 24, 8, 7, 6), (-1, 8, 24, 6, 6)):
        for name, fields, n in (("x1", pl.ds(1, 4), n1), ("xr", 0, nr)):
            s_at, d_at = (pl.ds(src - n, n), pl.ds(dst - n, n)) if d == 1 else (pl.ds(src, n), pl.ds(dst, n))
            plan((name, d), a1.at[fields, s_at, :, cols1], a1.at[fields, d_at, :, cols1], d, 0)
    for dx, dy in AROUND:
        e = (dy + 1) // 2
        if dy and dx == 0:
            plan(("y0", dx, dy), send0.at[e], recv0.at[e], dx, dy)
        if dy and dx:
            plan(("c0", dx, dy), corner.at[e, (dx + 1) // 2], recvc.at[e, (dx + 1) // 2], dx, dy)
        if dy:
            plan(("y1", dx, dy), send1.at[e], recv1.at[e, dx + 1], dx, dy)
            plan(("yr", dx, dy), sendr.at[e], recvr.at[e, dx + 1], dx, dy)
        plan(("k3", dx, dy), sendk, recvk.at[dx + 1, dy + 1], dx, dy)
        plan(("r3", dx, dy), send3, recv3.at[dx + 1, dy + 1], dx, dy)
        pairs = pl.ds(2 if dx == 1 else 0, 2 if dx else 4)
        plan(("e2", dx, dy), send2.at[pairs], recv2.at[dx + 1, dy + 1, pairs], dx, dy)
    for dy in (1, -1):
        plan(("y4", dy), pack4, side4.at[(dy + 1) // 2], 0, dy)
    for n, dx in enumerate(far):
        plan(("x4", dx), pack4.at[2 * REACH], pack4.at[n], dx, 0)
        plan(("xv", dx), widev.at[0], recvvx.at[n], dx, 0)
    for n, dx in enumerate((1, -1)):
        plan(("x3", dx), widev.at[pl.ds(1, 2)], recv3x.at[n], dx, 0)
    assert len(transfers) <= NSEM

    def tell(word):
        for e, dx in enumerate((2, -2)):

            def go(e=e, dx=dx):
                pl.semaphore_signal(known.at[word, e], inc=1, device_id=(mx + dx, my), device_id_type=MESH)

            when(there(dx), go)

    def hear(word):
        for e, dx in enumerate((2, -2)):
            when(there(-dx), lambda e=e: pl.semaphore_wait(known.at[word, e], 1))

    def zero(ref, *index):
        ref[index] = jnp.zeros(ref[index].shape, F32)

    @pl.when(mx == 0)
    def _():
        l0.a[:, 0:4] = jnp.zeros((5, 4, NZ, 384), F32)
        l1.a[:, 0:8] = jnp.zeros((5, 8, NZ, 256), F32)
        recv3x[0] = jnp.zeros((2, NZ, 128), F32)

    @pl.when(mx == gx - 1)
    def _():
        l0.a[:, 36:40] = jnp.zeros((5, 4, NZ, 384), F32)
        l1.a[:, 24:32] = jnp.zeros((5, 8, NZ, 256), F32)
        recv3x[1] = jnp.zeros((2, NZ, 128), F32)

    for n, dx in enumerate(far):

        @pl.when(jnp.logical_not(there(-dx)))
        def _(n=n):
            pack4[n] = jnp.zeros((NZ, 128), F32)
            recvvx[n] = jnp.zeros((NZ, 128), F32)

    for copy in loads:
        copy.wait()

    def widen(h, c):
        for f in range(4):
            wide[h, f] = raw_c[h, f].reshape(256, 128).astype(F32)
        top = pl.ds(224, 32)
        wide[h, 0, top] = wide[h, 0, top] + wide[h, 3, top]
        wide[h, 3, top] = jnp.zeros((32, 128), F32)
        return c

    for h in range(2):
        widen(h, 0)

    def turn(i):
        for h in range(2):
            cols = slice(128 * h, 128 * h + 128)
            l0.a[0, 4 + i, :, cols] = raw_s.at[h].reshape(256, 128)[pl.ds(i, NZ, stride=32), :]
            for f in range(4):
                l0.a[1 + f, 4 + i, :, cols] = wide.at[h, f][pl.ds(i, NZ, stride=32), :]

    for i in range(R0):
        turn(i)

    def pack(a, fields, own, count, width, last, dst):
        per = 128 // width
        lane = lanes_of((NZ, 128))
        for e in range(2):
            at = pl.ds(last, 128) if e == 1 else pl.ds(0, 128)
            for g in range(count // per):
                total = None
                for j in range(per):
                    row = a[fields, own + g * per + j, :, at]
                    shift = (width * j + (width if e == 1 else 0)) % 128
                    row = pltpu.roll(row, shift, row.ndim - 1) if shift else row
                    total = row if total is None else jnp.where(lane // width == j, row, total)
                dst[e, g] = total

    has_left, has_right = my > 0, my < gy - 1

    def unpack(part, a, fields, own, count, width, last, rows):
        lane = lanes_of((NZ, 128))
        for i in rows:
            dx = -1 if i < 0 else (1 if i >= count else 0)
            keep_r, keep_l = has_right, has_left
            if dx:
                keep_r, keep_l = keep_r & there(dx), keep_l & there(dx)
            sides = []
            for e in range(2):
                values, place = part(e, dx, i - dx * count)
                shift = (128 - width * (place + e)) % 128
                sides.append(pltpu.roll(values, shift, values.ndim - 1) if shift else values)
            row = jnp.where((lane < width) & keep_r, sides[0], jnp.where((lane >= 128 - width) & keep_l, sides[1], 0.0))
            a[fields, own + i, :, pl.ds(last, 128)] = row

    all_fields, coefs = slice(0, 5), slice(1, 5)
    lane = lanes_of((NZ, 128))
    sides = [p for p in AROUND if p[1]]

    def names(name, places=AROUND):
        return [(name, *p) for p in places]

    pack(l0.a, all_fields, 4, 32, 4, 128, send0)
    for e in range(2):
        for d in range(2):
            total = None
            for f in range(5):
                shift = (16 * f - (112 if d else 0)) % 128
                part = send0[e, 0, f]
                part = pltpu.roll(part, shift, 1) if shift else part
                total = part if total is None else jnp.where(lane < 16 * f, total, part)
            corner[e, d] = total
    l0.coarsen(0, 16, l1)
    pack(l1.a, coefs, 8, 16, 8, 0, send1)
    pl.semaphore_wait(barrier, count)
    first = [("x0", 1), ("x0f", 1), ("x0", -1)] + names("y0", [(0, 1), (0, -1)]) + names("c0", [p for p in sides if p[0]])
    send(first)

    second = [("x1", 1), ("x1", -1)] + names("y1", sides)
    send(second)
    l1.coarsen(0, 8, l2)
    l2.coarsen(0, 4, l3)

    def pack3(row):
        total = row(0)
        for j in range(1, 4):
            part = row(j)
            total = jnp.where(lane < 32 * j, total, pltpu.roll(part, 32 * j, part.ndim - 1))
        return total

    sendk[...] = pack3(lambda j: l3.a[1:5, 4 + j])
    send(names("k3"))
    l3.coarsen(0, 2, l4)
    total = l4.a[1, 12]
    for q in range(1, 8):
        total = jnp.where(lane < 16 * q, total, pltpu.roll(l4.a[1 + q // 2, 12 + q % 2], 16 * q, 1))
    pack4[2 * REACH] = total

    def part0(e, dx, j):
        if dx == 0:
            return recv0[e, 0], j
        j = j - 28 if dx < 0 else j
        values = recvc[e, (1 - dx) // 2]
        return jnp.stack([pltpu.roll(values, 128 - 16 * f, 1) if f else values for f in range(5)]), j

    beside = first[3:5]
    arrive(beside)
    unpack(part0, l0.a, all_fields, 4, 32, 4, 256, range(32))
    l0.diagonal(1, 32)
    l0.first(1, 32, l0.va)
    l0.sweep(2, 31, l0.va, l0.vb)
    l0.restrict_residual(4, 30, l0.vb, l1)
    arrive(first[:3] + first[5:])
    tell(0)
    unpack(part0, l0.a, all_fields, 4, 32, 4, 256, [*range(-4, 0), *range(32, 35)])
    for lo, hi in ((-2, 1), (32, 34)):
        l0.diagonal(lo, hi)
    for lo, hi in ((-2, 1), (32, 34)):
        l0.first(lo, hi, l0.va)
    for lo, hi in ((-1, 2), (31, 33)):
        l0.sweep(lo, hi, l0.va, l0.vb)
    for lo, hi in ((0, 4), (30, 32)):
        l0.restrict_residual(lo, hi, l0.vb, l1)
    pack(l1.a, 0, 8, 16, 8, 0, sendr)
    third = [("xr", 1), ("xr", -1)] + names("yr", sides)
    send(third)
    later = [("x0b", 1), ("x0c", 1), ("x0d", 1), ("x0b", -1)]
    send(later)

    arrive(second)
    hear(0)
    tell(1)
    unpack(lambda e, dx, j: (recv1[e, 1 - dx, 0], j), l1.a, coefs, 8, 16, 8, 128, range(-7, 22))
    l1.diagonal(-6, 22)
    l1.coarsen(-3, 11, l2, fx_low=-4)
    l2.diagonal(-3, 11)

    def spread3(own, src, a, fields):
        for px in (-1, 0, 1):
            mid, from_r, from_l = own if px == 0 else src[1 - px, 1], src[1 - px, 0], src[1 - px, 2]
            for j in range(4):
                parts = []
                for values, shift in ((mid, -32 * j), (from_r, 32 - 32 * j), (from_l, 96 - 32 * j)):
                    parts.append(pltpu.roll(values, shift % 128, values.ndim - 1) if shift % 128 else values)
                row = jnp.where((lane < 64) & has_right, parts[1], jnp.where((lane >= 96) & has_left, parts[2], 0.0))
                row = jnp.where(lane < 32, parts[0], row)
                if px:
                    row = jnp.where(there(px), row, 0.0)
                a[fields, 4 + 4 * px + j] = row

    arrive(names("k3"))
    spread3(sendk[...], recvk, l3.a, coefs)
    l3.diagonal(-3, 7)
    l3.coarsen(-1, 2, l4)
    l4.diagonal(0, 2)

    arrive(third)
    unpack(lambda e, dx, j: (recvr[e, 1 - dx, 0], j), l1.a, 0, 8, 16, 8, 128, range(-6, 22))
    l1.first(-6, 22, l1.va)
    l1.sweep(-5, 21, l1.va, l1.vb)
    l1.restrict_residual(-4, 20, l1.vb, l2)
    l2.first(-2, 10, l2.va)
    l2.sweep(-1, 9, l2.va, l2.vb)
    l2.restrict_residual(0, 8, l2.vb, l3)

    send3[...] = pack3(lambda j: l3.a[0, 4 + j])
    send(names("r3"))
    for n in range(4):
        send2[n, 0] = jnp.where(lane < 64, l2.a[0, 8 + 2 * n], pltpu.roll(l2.a[0, 9 + 2 * n], 64, 1))
        send2[n, 1] = jnp.where(lane < 64, l2.vb[8 + 2 * n], pltpu.roll(l2.vb[9 + 2 * n], 64, 1))
    hear(1)
    send([("x4", dx) for dx in far])
    send(names("e2"))

    arrive(names("r3"))
    spread3(send3[...], recv3, l3.a, 0)
    l3.first(-2, 6, l3.va)
    l3.sweep(-1, 5, l3.va, l3.vb)
    l3.restrict_residual(0, 4, l3.vb, l4)
    l4.first(0, 2, l4.va)

    def two(ref, i):
        return jnp.where((lane < 48) | (lane >= 112), ref[i], pltpu.roll(ref[i + 1], 64, 1))

    widev[0] = two(l4.va, 12)
    send([("xv", dx) for dx in far])
    for n in range(2):
        widev[1 + n] = two(l3.vb, 4 + 2 * n)
    send([("x3", 1), ("x3", -1)])

    def spread_two(both, ref, i):
        ref[i] = both
        ref[i + 1] = pltpu.roll(both, 64, both.ndim - 1)

    arrive([("x4", dx) for dx in far])
    send([("y4", 1), ("y4", -1)])

    arrive(later)
    for lo, hi in ((-3, -2), (34, 35)):
        l0.diagonal(lo, hi)
        l0.first(lo, hi, l0.va)
    for lo, hi in ((-2, -1), (33, 34)):
        l0.sweep(lo, hi, l0.va, l0.vb)
    arrive(names("e2"))
    for px in (-1, 0, 1):
        for n in (range(2, 4) if px < 0 else range(2) if px else range(4)):
            mid = send2[n] if px == 0 else recv2[1 - px, 1, n]
            from_r, from_l = recv2[1 - px, 0, n], recv2[1 - px, 2, n]
            zero = jnp.zeros_like(mid)
            from_r, from_l = jnp.where(has_right, from_r, zero), jnp.where(has_left, from_l, zero)
            even = jnp.where(lane < 64, mid, pltpu.roll(jnp.where(lane < 32, from_r, from_l), 64, 2))
            odd = jnp.where(lane < 64, pltpu.roll(mid, 64, 2), jnp.where(lane < 96, from_r, from_l))
            for j, row in enumerate((even, odd)):
                if px:
                    row = jnp.where(there(px), row, zero)
                i = 8 + 8 * px + 2 * n + j
                l2.a[0, i] = row[0]
                l2.vb[i] = row[1]

    arrive([("y4", 1), ("y4", -1)])
    keep_r, keep_l = (lane < 64) & has_right, (lane >= 64) & has_left
    for n, dx in enumerate(far + [0]):
        i = 12 - 2 * dx
        own, from_r, from_l = pack4[n], side4[0, n], side4[1, n]
        for q in range(8):
            parts = [pltpu.roll(p, b % 128, 1) if b % 128 else p for p, b in ((own, -16 * q), (from_r, 16 - 16 * q), (from_l, -16 - 16 * q))]
            row = jnp.where(lane < 16, parts[0], jnp.where(keep_r, parts[1], jnp.where(keep_l, parts[2], 0.0)))
            l4.a[1 + q // 2, i + q % 2] = row
    l4.diagonal(-11, 13)
    l4.coarsen(-5, 6, l5, fx_low=-6)
    l5.diagonal(-5, 6)
    late = ("xv", "x3")
    grouped([n for n in transfers if n[0] not in late], lambda c: c.wait_send(), 1)

    arrive([("xv", dx) for dx in far])
    for n, dx in list(enumerate(far)) + [(None, 0)]:
        spread_two(widev[0] if dx == 0 else recvvx[n], l4.va, 12 - 2 * dx)

    def body(i, k):
        l4.a[0, pl.ds(i + 12, k)] = l4.rows(l4.va, i, k) * l4.rows(l4.d, i, k) * (1 / DAMPING)

    chunks(-11, 13, 8, body)
    l4.sweep(-11, 13, l4.va, l4.vb)
    l4.restrict_residual(-10, 12, l4.vb, l5)

    l5.first(-5, 6, l5.va)
    l5.sweep(-4, 5, l5.va, l5.vb)
    l5.sweep(-3, 4, l5.vb, l5.va)
    l5.sweep(-2, 3, l5.va, l5.vb)

    l4.correct(-4, 6, l4.vb, l5, l5.vb, l4.va)
    l4.sweep(-3, 5, l4.va, l4.vb)
    l4.sweep(-2, 4, l4.vb, l4.va)

    arrive([("x3", 1), ("x3", -1)])
    for src, dx in ((recv3x.at[0], 1), (recv3x.at[1], -1)):
        for n in range(2):
            spread_two(src[n], l3.vb, 4 - 4 * dx + 2 * n)
    l3.correct(-4, 8, l3.vb, l4, l4.va, l3.va)
    l3.sweep(-3, 7, l3.va, l3.vb)
    l3.sweep(-2, 6, l3.vb, l3.va)

    l2.correct(-4, 12, l2.vb, l3, l3.va, l2.va)
    l2.sweep(-3, 11, l2.va, l2.vb)
    l2.sweep(-2, 10, l2.vb, l2.va)

    l1.correct(-4, 20, l1.vb, l2, l2.va, l1.va)
    l1.sweep(-2, 18, l1.va, l1.vb)
    l1.sweep(-1, 17, l1.vb, l1.va)

    l0.correct(-2, 34, l0.vb, l1, l1.va, l0.va)
    l0.sweep(-1, 33, l0.va, l0.vb)

    def last(n, c):
        for q in range(2):
            i = 8 * n + 4 * q
            mid, total = l0.beside(l0.vb, i, 4)
            new = (1 - DAMPING) * mid + l0.rows(l0.rd, i, 4) * total
            for j in range(4):
                for h in range(2):
                    out_v.at[h].reshape(256, 128)[pl.ds(i + j, NZ, stride=32), :] = new[j, :, 128 * h : 128 * h + 128]
        return c

    for n in range(4):
        last(n, 0)
        for h in range(2):
            rows, cols = pl.ds(8 * n, 8), pl.ds(128 * h, 128)
            pltpu.make_async_copy(out_v.at[h, :, rows], field.at[:, rows, cols], store_sem.at[n, h]).start()

    grouped([n for n in transfers if n[0] in late], lambda c: c.wait_send(), 1)
    for n in range(4):
        for h in range(2):
            rows, cols = pl.ds(8 * n, 8), pl.ds(128 * h, 128)
            pltpu.make_async_copy(out_v.at[h, :, rows], field.at[:, rows, cols], store_sem.at[n, h]).wait()


def solution(mesh):
    gx, gy = mesh.shape["gx"], mesh.shape["gy"]
    def step(*args):
        scratch = [
            pltpu.VMEM((2, NZ, R0, 128), F32),
            pltpu.VMEM((2, 4, NZ, R0, 128), jnp.bfloat16),
            pltpu.VMEM((2, 4, NZ * R0, 128), F32),
            pltpu.VMEM((2, NZ, R0, 128), F32),
        ]
        for rows, cols in zip(ROWS, LANES):
            scratch.append(pltpu.VMEM((5, rows, NZ, cols), F32))
            scratch += [pltpu.VMEM((rows, NZ, cols), F32)] * 4
        scratch += [
            pltpu.VMEM((2, 1, 5, NZ, 128), F32),
            pltpu.VMEM((2, 1, 5, NZ, 128), F32),
            pltpu.VMEM((2, 2, NZ, 128), F32),
            pltpu.VMEM((2, 2, NZ, 128), F32),
            pltpu.VMEM((2, 1, 4, NZ, 128), F32),
            pltpu.VMEM((2, 3, 1, 4, NZ, 128), F32),
            pltpu.VMEM((2, 1, NZ, 128), F32),
            pltpu.VMEM((2, 3, 1, NZ, 128), F32),
            pltpu.VMEM((NZ, 128), F32),
            pltpu.VMEM((3, 3, NZ, 128), F32),
            pltpu.VMEM((4, NZ, 128), F32),
            pltpu.VMEM((3, 3, 4, NZ, 128), F32),
            pltpu.VMEM((4, 2, NZ, 128), F32),
            pltpu.VMEM((3, 3, 4, 2, NZ, 128), F32),
            pltpu.VMEM((2 * REACH + 1, NZ, 128), F32),
            pltpu.VMEM((2, 2 * REACH + 1, NZ, 128), F32),
            pltpu.VMEM((3, NZ, 128), F32),
            pltpu.VMEM((2 * REACH, NZ, 128), F32),
            pltpu.VMEM((2, 2, NZ, 128), F32),
            pltpu.SemaphoreType.DMA((2, 5)),
            pltpu.SemaphoreType.DMA((4, 2)),
            pltpu.SemaphoreType.DMA((NSEM,)),
            pltpu.SemaphoreType.DMA((NSEM,)),
            pltpu.SemaphoreType.REGULAR((2, 2)),
        ]

        def body(*refs):
            kernel(gx, gy, *refs)

        return pl.pallas_call(
            body,
            out_shape=jax.ShapeDtypeStruct((NZ, R0, C0), F32),
            in_specs=[pl.BlockSpec(memory_space=pl.ANY)] * 5,
            out_specs=pl.BlockSpec(memory_space=pl.ANY),
            scratch_shapes=scratch,
            compiler_params=pltpu.CompilerParams(
                collective_id=0, has_side_effects=True, vmem_limit_bytes=60 * 2**20
            ),
        )(*args)

    placed = P(None, "gx", "gy")
    return jax.shard_map(step, mesh=mesh, in_specs=(placed,) * 5, out_specs=placed, check_vma=False)
```

```python
import jax
import jax.numpy as jnp
from jax import lax
from jax.experimental import pallas as pl
from jax.experimental.pallas import tpu as pltpu
from jax.sharding import PartitionSpec as P

DAMPING = 0.8
F32 = jnp.float32
MESH = pl.DeviceIdType.MESH
NZ, R0, C0 = 8, 32, 256
OWN = (4, 8, 8, 4, 12, 6)
ROWS = (40, 32, 24, 12, 26, 12)
LANES = (384, 256, 128, 128, 128, 128)
REACH = 6
NSEM = 96
AROUND = [(dx, dy) for dx in (0, 1, -1) for dy in (0, 1, -1) if dx or dy]


def lanes_of(shape):
    return lax.broadcasted_iota(jnp.int32, shape, len(shape) - 1)


def left(values):
    return pltpu.roll(values, values.shape[-1] - 1, values.ndim - 1)


def right(values):
    return pltpu.roll(values, 1, values.ndim - 1)


def above(values):
    return pltpu.roll(values, values.shape[-2] - 1, values.ndim - 2)


def below(values):
    return pltpu.roll(values, 1, values.ndim - 2)


def take(values, index):
    rows = values.size // 128
    flat = jnp.take_along_axis(values.reshape(rows, 128), jnp.broadcast_to(index, (rows, 128)), axis=1)
    return flat.reshape(values.shape)


def squeeze(first, second, odd=False):
    lane = lanes_of((1, 128))
    index = (2 * lane + (1 if odd else 0)) & 127
    one = take(first, index)
    if second is None:
        return one
    return jnp.where(lanes_of(first.shape) < 64, one, take(second, index))


def pair(values):
    return values + pltpu.roll(values, 127, values.ndim - 1)


def squeeze_wide(values, odd=False, sums=True):
    parts = [values[..., 128 * j : 128 * j + 128] for j in range(values.shape[-1] // 128)]
    if sums:
        parts = [pair(p) for p in parts]
    return squeeze(parts[0], parts[1] if len(parts) > 1 else None, odd)


def stretch_index(kind):
    lane = lanes_of((1, 128))
    half = lane // 2
    if kind == "low":
        return half
    if kind == "high":
        return half + 64
    split = 64 if kind == "ends" else 96
    return half + jnp.where(lane >= split, 64, 0)


def chunks(lo, hi, step, body):
    for i in range(lo, hi, step):
        body(i, min(step, hi - i))


class Level:
    def __init__(self, level, a, d, rd, va, vb):
        self.level, self.a, self.d, self.rd, self.va, self.vb = level, a, d, rd, va, vb
        self.own = OWN[level]
        self.step = (38, 32, 24, 12, 26, 12)[level]

    def rows(self, ref, i, k):
        return ref[pl.ds(i + self.own, k)]

    def field(self, f, i, k):
        return self.a[f, pl.ds(i + self.own, k)]

    def diagonal(self, lo, hi):
        def body(i, k):
            kappa = self.field(1, i, k)
            fx, fxl, fy, fz = self.field(2, i, k), self.field(2, i - 1, k), self.field(3, i, k), self.field(4, i, k)
            d = kappa + fx + fxl + fy + right(fy) + fz + below(fz)
            self.d[pl.ds(i + self.own, k)] = d
            self.rd[pl.ds(i + self.own, k)] = jnp.where(kappa > 0, DAMPING / d, 0.0)

        chunks(lo, hi, self.step, body)

    def beside(self, v, i, k):
        c = self.rows(v, i, k)
        fx, fxl, fy, fz = self.field(2, i, k), self.field(2, i - 1, k), self.field(3, i, k), self.field(4, i, k)
        along_x = fx * self.rows(v, i + 1, k) + fxl * self.rows(v, i - 1, k)
        along_y = fy * left(c) + right(fy * c)
        along_z = fz * above(c) + below(fz * c)
        return c, (self.field(0, i, k) + along_x) + (along_y + along_z)

    def first(self, lo, hi, out):
        def body(i, k):
            out[pl.ds(i + self.own, k)] = self.rows(self.rd, i, k) * self.field(0, i, k)

        chunks(lo, hi, self.step, body)

    def sweep(self, lo, hi, v, out):
        def body(i, k):
            c, total = self.beside(v, i, k)
            new = (1 - DAMPING) * c + self.rows(self.rd, i, k) * total
            out[pl.ds(i + self.own, k)] = new

        chunks(lo, hi, self.step, body)

    def beside_values(self, v, lo):
        c, k = v[1:-1], v.shape[0] - 2
        fx, fxl, fy, fz = self.field(2, lo, k), self.field(2, lo - 1, k), self.field(3, lo, k), self.field(4, lo, k)
        along_x = fx * v[2:] + fxl * v[:-2]
        along_y = fy * left(c) + right(fy * c)
        along_z = fz * above(c) + below(fz * c)
        return c, (self.field(0, lo, k) + along_x) + (along_y + along_z)

    def first_values(self, lo, hi):
        return self.rows(self.rd, lo, hi - lo) * self.field(0, lo, hi - lo)

    def sweep_values(self, v, lo):
        c, total = self.beside_values(v, lo)
        return (1 - DAMPING) * c + self.rows(self.rd, lo, c.shape[0]) * total

    def down(self, lo, hi, v, coarse):
        v = self.sweep_values(v, lo + 1)
        self.vb[pl.ds(lo + 1 + self.own, v.shape[0])] = v
        c, total = self.beside_values(v, lo + 2)
        residual = total - self.rows(self.d, lo + 2, c.shape[0]) * c
        m = c.shape[0] // 2
        residual = residual.reshape(m, 2, *residual.shape[1:])
        coarse.a[0, pl.ds((lo + 2) // 2 + coarse.own, m)] = squeeze_wide(residual[:, 0] + residual[:, 1]) * 0.25

    def up(self, v, lo, hi, cut=0):
        m = v.shape[0]
        if self.level == 1:
            parts = [take(v, stretch_index("low")), take(v, stretch_index("high"))]
        else:
            parts = [take(v, stretch_index("late"))]
        parts = [jnp.broadcast_to(p[:, None], (m, 2, NZ, 128)).reshape(2 * m, NZ, 128) for p in parts]
        v = self.rows(self.vb, lo, hi - lo) + (parts[0] if len(parts) == 1 else jnp.concatenate(parts, axis=2))
        v = v[cut : v.shape[0] - cut]
        return self.sweep_values(self.sweep_values(v, lo + cut + 1), lo + cut + 2)

    def restrict_residual(self, lo, hi, v, coarse):
        def body(n, m):
            k = 2 * m
            i = 2 * n
            c, total = self.beside(v, i, k)
            residual = total - self.rows(self.d, i, k) * c
            residual = residual[..., : min(residual.shape[-1], 256)]
            residual = residual.reshape(m, 2, *residual.shape[1:])
            coarse.a[0, pl.ds(n + coarse.own, m)] = fit(squeeze_wide(residual[:, 0] + residual[:, 1]) * 0.25, coarse)

        chunks(lo // 2, hi // 2, self.step // 2, body)

    def coarsen(self, lo, hi, coarse, fx_low=None):
        def body(n, m):
            both = [self.field(f, 2 * n, 2 * m)[..., : min(self.a.shape[-1], 256)] for f in (1, 2, 3, 4)]
            both = [b.reshape(m, 2, *b.shape[1:]) for b in both]
            kappa, fx, fy, fz = both
            at = pl.ds(n + coarse.own, m)
            coarse.a[1, at] = fit(squeeze_wide(kappa[:, 0] + kappa[:, 1]) * 0.25, coarse)
            coarse.a[2, at] = fit(squeeze_wide(fx[:, 1]) * 0.25, coarse)
            coarse.a[3, at] = fit(squeeze_wide(fy[:, 0] + fy[:, 1], odd=True, sums=False) * 0.25, coarse)
            coarse.a[4, at] = fit(squeeze_wide(fz[:, 0] + fz[:, 1]) * 0.25, coarse)

        chunks(lo, hi, self.step // 2, body)
        if fx_low is not None:
            fx = self.field(2, 2 * fx_low + 1, 1)
            coarse.a[2, pl.ds(fx_low + coarse.own, 1)] = squeeze_wide(fx) * 0.25

    def correct(self, lo, hi, v, coarse, c, out):
        def body(n, m):
            values = c[pl.ds(n + coarse.own, m)]
            if self.level == 0:
                first, second = values[..., :128], values[..., 128:]
                fine = [take(first, stretch_index("low")), take(first, stretch_index("high")), take(second, stretch_index("ends"))]
            elif self.level == 1:
                fine = [take(values, stretch_index("low")), take(values, stretch_index("high"))]
            else:
                fine = [take(values, stretch_index("late"))]
            for j, part in enumerate(fine):
                cols = slice(128 * j, 128 * j + 128)
                at = pl.ds(2 * n + self.own, 2 * m)
                spread = jnp.broadcast_to(part[:, None], (m, 2, NZ, 128)).reshape(2 * m, NZ, 128)
                out[at, :, cols] = v[at, :, cols] + spread

        chunks(lo // 2, hi // 2, max(self.step // 2, 1), body)


def fit(values, coarse):
    if coarse.level == 1:
        return jnp.concatenate([values, jnp.zeros_like(values)], axis=-1)
    return values


def kernel(gx, gy, source, kappa_sq, face_x, face_y, face_z, field, *refs):
    refs = list(refs)

    def get(n):
        out = refs[:n]
        del refs[:n]
        return out

    raw_s, raw_c, wide, out_v = get(4)
    levels = []
    for n in range(6):
        levels.append(Level(n, *get(5)))
    send0, recv0, corner, recvc, send1, recv1, sendr, recvr = get(8)
    send3, recv3, sendk, recvk, send2, recv2 = get(6)
    pack4, side4, widev, recvvx, recv3x = get(5)
    load_sem, store_sem, ssem, rsem, known = get(5)
    l0, l1, l2, l3, l4, l5 = levels

    mx, my = lax.axis_index("gx"), lax.axis_index("gy")

    def there(dx):
        if dx == 0:
            return None
        return mx + dx < gx if dx > 0 else mx + dx >= 0

    def when(cond, action):
        if cond is None:
            action()
        else:
            pl.when(cond)(action)

    far = [s * k for k in range(REACH, 0, -1) for s in (1, -1)]

    barrier = pltpu.get_barrier_semaphore()
    partners = AROUND
    count = 0
    for dx in (0, 1, -1):
        group = [p for p in partners if p[0] == dx]

        def greet(group=group):
            for px, py in group:
                ids = (mx + px, lax.rem(my + py + gy, gy))
                pl.semaphore_signal(barrier, inc=1, device_id=ids, device_id_type=MESH)

        when(there(dx), greet)
        count = count + (len(group) if dx == 0 else jnp.where(there(dx), len(group), 0))

    loads = []
    for h in range(2):
        cols = pl.ds(128 * h, 128)
        loads.append(pltpu.make_async_copy(source.at[:, :, cols], raw_s.at[h], load_sem.at[h, 0]))
        for f, ref in enumerate((kappa_sq, face_x, face_y, face_z)):
            loads.append(pltpu.make_async_copy(ref.at[:, :, cols], raw_c.at[h, f], load_sem.at[h, f + 1]))
    for copy in loads:
        copy.start()

    transfers = {}

    def plan(name, src, dst, dx, dy):
        transfers[name] = (src, dst, dx, dy, len(transfers))

    def copy_of(name):
        src, dst, dx, dy, n = transfers[name]
        ids = (mx + dx, lax.rem(my + dy + gy, gy))
        return pltpu.make_async_remote_copy(
            src_ref=src, dst_ref=dst, send_sem=ssem.at[n], recv_sem=rsem.at[n], device_id=ids, device_id_type=MESH
        )

    def grouped(names, action, sign):
        by = {}
        for name in names:
            by.setdefault(transfers[name][2], []).append(name)
        reach = max(abs(dx) for dx in by)

        def group(dx):
            for name in by[dx]:
                action(copy_of(name))

        def every():
            for dx in by:
                group(dx)

        def some():
            for dx in by:
                when(there(sign * dx), lambda dx=dx: group(dx))

        if reach == 0:
            every()
        else:
            inside = (mx >= reach) & (mx < gx - reach)
            pl.when(inside)(every)
            pl.when(jnp.logical_not(inside))(some)

    def send(names):
        grouped(names, lambda c: c.start(), 1)

    def arrive(names):
        grouped(names, lambda c: c.wait_recv(), -1)

    a0, a1 = l0.a, l1.a
    cols, cols1 = pl.ds(0, C0), pl.ds(0, 128)

    def rows0(name, fields, src, dst, rows, d):
        plan((name, d), a0.at[fields, pl.ds(src, rows), :, cols], a0.at[fields, pl.ds(dst, rows), :, cols], d, 0)

    rows0("x0", pl.ds(0, 5), 34, 2, 2, 1)
    rows0("x0f", 2, 33, 1, 1, 1)
    rows0("x0", pl.ds(0, 5), 4, 36, 2, -1)
    rows0("x0b", pl.ds(0, 2), 33, 1, 1, 1)
    rows0("x0c", pl.ds(3, 2), 33, 1, 1, 1)
    rows0("x0d", 2, 32, 0, 1, 1)
    rows0("x0b", pl.ds(0, 5), 6, 38, 1, -1)
    for d, src, dst, n1, nr in ((1, 24, 8, 7, 6), (-1, 8, 24, 6, 6)):
        for name, fields, n in (("x1", pl.ds(1, 4), n1), ("xr", 0, nr)):
            s_at, d_at = (pl.ds(src - n, n), pl.ds(dst - n, n)) if d == 1 else (pl.ds(src, n), pl.ds(dst, n))
            plan((name, d), a1.at[fields, s_at, :, cols1], a1.at[fields, d_at, :, cols1], d, 0)
    for dx, dy in AROUND:
        e = (dy + 1) // 2
        if dy and dx == 0:
            plan(("y0", dx, dy), send0.at[e], recv0.at[e], dx, dy)
        if dy and dx:
            plan(("c0", dx, dy), corner.at[e, (dx + 1) // 2], recvc.at[e, (dx + 1) // 2], dx, dy)
        if dy:
            plan(("y1", dx, dy), send1.at[e], recv1.at[e, dx + 1], dx, dy)
            plan(("yr", dx, dy), sendr.at[e], recvr.at[e, dx + 1], dx, dy)
        plan(("k3", dx, dy), sendk, recvk.at[dx + 1, dy + 1], dx, dy)
        plan(("r3", dx, dy), send3, recv3.at[dx + 1, dy + 1], dx, dy)
        pairs = pl.ds(2 if dx == 1 else 0, 2 if dx else 4)
        plan(("e2", dx, dy), send2.at[pairs], recv2.at[dx + 1, dy + 1, pairs], dx, dy)
    for dy in (1, -1):
        plan(("y4", dy), pack4, side4.at[(dy + 1) // 2], 0, dy)
    for n, dx in enumerate(far):
        plan(("x4", dx), pack4.at[2 * REACH], pack4.at[n], dx, 0)
        plan(("xv", dx), widev.at[0], recvvx.at[n], dx, 0)
    for n, dx in enumerate((1, -1)):
        plan(("x3", dx), widev.at[pl.ds(1, 2)], recv3x.at[n], dx, 0)
    assert len(transfers) <= NSEM

    def tell(word):
        for e, dx in enumerate((1, -1) if word == 0 else (2, -2)):

            def go(e=e, dx=dx):
                pl.semaphore_signal(known.at[word, e], inc=1, device_id=(mx + dx, my), device_id_type=MESH)

            when(there(dx), go)

    def hear(word):
        for e, dx in enumerate((1, -1) if word == 0 else (2, -2)):
            when(there(-dx), lambda e=e: pl.semaphore_wait(known.at[word, e], 1))

    def zero(ref, *index):
        ref[index] = jnp.zeros(ref[index].shape, F32)

    @pl.when(mx == 0)
    def _():
        l0.a[:, 0:4] = jnp.zeros((5, 4, NZ, 384), F32)
        l1.a[:, 0:8] = jnp.zeros((5, 8, NZ, 256), F32)
        recv3x[0] = jnp.zeros((2, NZ, 128), F32)

    @pl.when(mx == gx - 1)
    def _():
        l0.a[:, 36:40] = jnp.zeros((5, 4, NZ, 384), F32)
        l1.a[:, 24:32] = jnp.zeros((5, 8, NZ, 256), F32)
        recv3x[1] = jnp.zeros((2, NZ, 128), F32)

    for n, dx in enumerate(far):

        @pl.when(jnp.logical_not(there(-dx)))
        def _(n=n):
            pack4[n] = jnp.zeros((NZ, 128), F32)
            recvvx[n] = jnp.zeros((NZ, 128), F32)

    for copy in loads:
        copy.wait()

    def widen(h, c):
        for f in range(4):
            wide[h, f] = raw_c[h, f].reshape(256, 128).astype(F32)
        top = pl.ds(224, 32)
        wide[h, 0, top] = wide[h, 0, top] + wide[h, 3, top]
        wide[h, 3, top] = jnp.zeros((32, 128), F32)
        return c

    for h in range(2):
        widen(h, 0)

    def turn(i):
        for h in range(2):
            cols = slice(128 * h, 128 * h + 128)
            l0.a[0, 4 + i, :, cols] = raw_s.at[h].reshape(256, 128)[pl.ds(i, NZ, stride=32), :]
            for f in range(4):
                l0.a[1 + f, 4 + i, :, cols] = wide.at[h, f][pl.ds(i, NZ, stride=32), :]

    for i in range(R0):
        turn(i)

    def pack(a, fields, own, count, width, last, dst):
        per = 128 // width
        lane = lanes_of((NZ, 128))
        for e in range(2):
            at = pl.ds(last, 128) if e == 1 else pl.ds(0, 128)
            for g in range(count // per):
                total = None
                for j in range(per):
                    row = a[fields, own + g * per + j, :, at]
                    shift = (width * j + (width if e == 1 else 0)) % 128
                    row = pltpu.roll(row, shift, row.ndim - 1) if shift else row
                    total = row if total is None else jnp.where(lane // width == j, row, total)
                dst[e, g] = total

    has_left, has_right = my > 0, my < gy - 1

    def unpack(part, a, fields, own, count, width, last, rows):
        lane = lanes_of((NZ, 128))
        for i in rows:
            dx = -1 if i < 0 else (1 if i >= count else 0)
            keep_r, keep_l = has_right, has_left
            if dx:
                keep_r, keep_l = keep_r & there(dx), keep_l & there(dx)
            sides = []
            for e in range(2):
                values, place = part(e, dx, i - dx * count)
                shift = (128 - width * (place + e)) % 128
                sides.append(pltpu.roll(values, shift, values.ndim - 1) if shift else values)
            row = jnp.where((lane < width) & keep_r, sides[0], jnp.where((lane >= 128 - width) & keep_l, sides[1], 0.0))
            a[fields, own + i, :, pl.ds(last, 128)] = row

    all_fields, coefs = slice(0, 5), slice(1, 5)
    lane = lanes_of((NZ, 128))
    sides = [p for p in AROUND if p[1]]

    def names(name, places=AROUND):
        return [(name, *p) for p in places]

    first = [("x0", 1), ("x0f", 1), ("x0", -1)] + names("y0", [(0, 1), (0, -1)]) + names("c0", [p for p in sides if p[0]])
    pl.semaphore_wait(barrier, count)
    send(first[:3])
    pack(l0.a, all_fields, 4, 32, 4, 128, send0)
    for e in range(2):
        for d in range(2):
            total = None
            for f in range(5):
                shift = (16 * f - (112 if d else 0)) % 128
                part = send0[e, 0, f]
                part = pltpu.roll(part, shift, 1) if shift else part
                total = part if total is None else jnp.where(lane < 16 * f, total, part)
            corner[e, d] = total
    first = [("x0", 1), ("x0f", 1), ("x0", -1)] + names("y0", [(0, 1), (0, -1)]) + names("c0", [p for p in sides if p[0]])
    send(first[3:])
    l0.coarsen(0, 16, l1)
    pack(l1.a, coefs, 8, 16, 8, 0, send1)

    second = [("x1", 1), ("x1", -1)] + names("y1", sides)
    send(second)
    tell(0)
    l1.coarsen(0, 8, l2)
    l2.coarsen(0, 4, l3)

    def pack3(row):
        total = row(0)
        for j in range(1, 4):
            part = row(j)
            total = jnp.where(lane < 32 * j, total, pltpu.roll(part, 32 * j, part.ndim - 1))
        return total

    sendk[...] = pack3(lambda j: l3.a[1:5, 4 + j])
    send(names("k3"))
    l3.coarsen(0, 2, l4)
    total = l4.a[1, 12]
    for q in range(1, 8):
        total = jnp.where(lane < 16 * q, total, pltpu.roll(l4.a[1 + q // 2, 12 + q % 2], 16 * q, 1))
    pack4[2 * REACH] = total

    def part0(e, dx, j):
        if dx == 0:
            return recv0[e, 0], j
        j = j - 28 if dx < 0 else j
        values = recvc[e, (1 - dx) // 2]
        return jnp.stack([pltpu.roll(values, 128 - 16 * f, 1) if f else values for f in range(5)]), j

    beside = first[3:5]
    hear(0)
    tell(1)
    arrive(beside)
    unpack(part0, l0.a, all_fields, 4, 32, 4, 256, range(32))
    l0.diagonal(1, 32)
    l0.first(1, 32, l0.va)
    l0.sweep(2, 31, l0.va, l0.vb)
    l0.restrict_residual(4, 30, l0.vb, l1)
    close = names("y1", [(0, 1), (0, -1)])
    arrive(close)

    def part1(e, dx, j):
        return recv1[e, 1 - dx, 0], j

    unpack(part1, l1.a, coefs, 8, 16, 8, 128, range(16))
    l1.diagonal(1, 16)
    hear(1)
    tell(2)
    arrive(first[:3] + first[5:])
    unpack(part0, l0.a, all_fields, 4, 32, 4, 256, [*range(-4, 0), *range(32, 35)])
    for lo, hi in ((-2, 1), (32, 34)):
        l0.diagonal(lo, hi)
    for lo, hi in ((-2, 1), (32, 34)):
        l0.first(lo, hi, l0.va)
    for lo, hi in ((-1, 2), (31, 33)):
        l0.sweep(lo, hi, l0.va, l0.vb)
    for lo, hi in ((0, 4), (30, 32)):
        l0.restrict_residual(lo, hi, l0.vb, l1)
    pack(l1.a, 0, 8, 16, 8, 0, sendr)
    third = [("xr", 1), ("xr", -1)] + names("yr", sides)
    send(third)
    later = [("x0b", 1), ("x0c", 1), ("x0d", 1), ("x0b", -1)]

    arrive([n for n in second if n not in close])
    unpack(part1, l1.a, coefs, 8, 16, 8, 128, [*range(-7, 0), *range(16, 22)])
    l1.diagonal(-6, 1)
    l1.diagonal(16, 22)
    l1.coarsen(-3, 11, l2, fx_low=-4)
    l2.diagonal(-3, 11)

    def spread3(own, src, a, fields):
        for px in (-1, 0, 1):
            mid, from_r, from_l = own if px == 0 else src[1 - px, 1], src[1 - px, 0], src[1 - px, 2]
            for j in range(4):
                parts = []
                for values, shift in ((mid, -32 * j), (from_r, 32 - 32 * j), (from_l, 96 - 32 * j)):
                    parts.append(pltpu.roll(values, shift % 128, values.ndim - 1) if shift % 128 else values)
                row = jnp.where((lane < 64) & has_right, parts[1], jnp.where((lane >= 96) & has_left, parts[2], 0.0))
                row = jnp.where(lane < 32, parts[0], row)
                if px:
                    row = jnp.where(there(px), row, 0.0)
                a[fields, 4 + 4 * px + j] = row

    hear(2)
    send([("x4", dx) for dx in far])
    arrive(third)
    unpack(lambda e, dx, j: (recvr[e, 1 - dx, 0], j), l1.a, 0, 8, 16, 8, 128, range(-6, 22))
    l1.down(-6, 22, l1.first_values(-6, 22), l2)
    l2.down(-2, 10, l2.first_values(-2, 10), l3)

    send3[...] = pack3(lambda j: l3.a[0, 4 + j])
    send(names("r3"))
    for n in range(4):
        send2[n, 0] = jnp.where(lane < 64, l2.a[0, 8 + 2 * n], pltpu.roll(l2.a[0, 9 + 2 * n], 64, 1))
        send2[n, 1] = jnp.where(lane < 64, l2.vb[8 + 2 * n], pltpu.roll(l2.vb[9 + 2 * n], 64, 1))
    send(names("e2"))
    send(later)
    arrive(names("k3"))
    spread3(sendk[...], recvk, l3.a, coefs)
    l3.diagonal(-3, 7)
    l3.coarsen(-1, 2, l4)
    l4.diagonal(0, 2)

    arrive(names("r3"))
    spread3(send3[...], recv3, l3.a, 0)
    l3.down(-2, 6, l3.first_values(-2, 6), l4)
    l4.first(0, 2, l4.va)

    def two(ref, i):
        return jnp.where((lane < 48) | (lane >= 112), ref[i], pltpu.roll(ref[i + 1], 64, 1))

    widev[0] = two(l4.va, 12)
    send([("xv", dx) for dx in far])
    for n in range(2):
        widev[1 + n] = two(l3.vb, 4 + 2 * n)
    send([("x3", 1), ("x3", -1)])

    def spread_two(both, ref, i):
        ref[i] = both
        ref[i + 1] = pltpu.roll(both, 64, both.ndim - 1)

    arrive([("x4", dx) for dx in far])
    send([("y4", 1), ("y4", -1)])

    arrive(later)
    for lo, hi in ((-3, -2), (34, 35)):
        l0.diagonal(lo, hi)
        l0.first(lo, hi, l0.va)
    for lo, hi in ((-2, -1), (33, 34)):
        l0.sweep(lo, hi, l0.va, l0.vb)
    arrive(names("e2"))
    for px in (-1, 0, 1):
        for n in (range(2, 4) if px < 0 else range(2) if px else range(4)):
            mid = send2[n] if px == 0 else recv2[1 - px, 1, n]
            from_r, from_l = recv2[1 - px, 0, n], recv2[1 - px, 2, n]
            zero = jnp.zeros_like(mid)
            from_r, from_l = jnp.where(has_right, from_r, zero), jnp.where(has_left, from_l, zero)
            even = jnp.where(lane < 64, mid, pltpu.roll(jnp.where(lane < 32, from_r, from_l), 64, 2))
            odd = jnp.where(lane < 64, pltpu.roll(mid, 64, 2), jnp.where(lane < 96, from_r, from_l))
            for j, row in enumerate((even, odd)):
                if px:
                    row = jnp.where(there(px), row, zero)
                i = 8 + 8 * px + 2 * n + j
                l2.a[0, i] = row[0]
                l2.vb[i] = row[1]

    late = ("xv", "x3", "x4", "y4")
    grouped([n for n in transfers if n[0] not in late], lambda c: c.wait_send(), 1)
    arrive([("y4", 1), ("y4", -1)])
    keep_r, keep_l = (lane < 64) & has_right, (lane >= 64) & has_left
    for n, dx in enumerate(far + [0]):
        i = 12 - 2 * dx
        own, from_r, from_l = pack4[n], side4[0, n], side4[1, n]
        for q in range(8):
            parts = [pltpu.roll(p, b % 128, 1) if b % 128 else p for p, b in ((own, -16 * q), (from_r, 16 - 16 * q), (from_l, -16 - 16 * q))]
            row = jnp.where(lane < 16, parts[0], jnp.where(keep_r, parts[1], jnp.where(keep_l, parts[2], 0.0)))
            l4.a[1 + q // 2, i + q % 2] = row
    l4.diagonal(-11, 13)
    l4.coarsen(-5, 6, l5, fx_low=-6)
    l5.diagonal(-5, 6)

    arrive([("xv", dx) for dx in far])
    for n, dx in list(enumerate(far)) + [(None, 0)]:
        spread_two(widev[0] if dx == 0 else recvvx[n], l4.va, 12 - 2 * dx)

    v = l4.rows(l4.va, -12, 26)
    l4.a[0, pl.ds(1, 24)] = v[1:25] * l4.rows(l4.d, -11, 24) * (1 / DAMPING)
    l4.down(-12, 14, v, l5)

    v = l5.first_values(-5, 6)
    for lo in (-4, -3, -2):
        v = l5.sweep_values(v, lo)

    v = l4.up(v, -4, 6)
    arrive([("x3", 1), ("x3", -1)])
    for src, dx in ((recv3x.at[0], 1), (recv3x.at[1], -1)):
        for n in range(2):
            spread_two(src[n], l3.vb, 4 - 4 * dx + 2 * n)
    v = l3.up(v, -4, 8)
    v = l2.up(v, -4, 12)
    l1.va[pl.ds(l1.own - 1, 18)] = l1.up(v, -4, 20, 1)

    l0.correct(-2, 34, l0.vb, l1, l1.va, l0.va)
    l0.sweep(-1, 33, l0.va, l0.vb)

    def last(n, c):
        for q in range(2):
            i = 8 * n + 4 * q
            mid, total = l0.beside(l0.vb, i, 4)
            new = (1 - DAMPING) * mid + l0.rows(l0.rd, i, 4) * total
            for j in range(4):
                for h in range(2):
                    out_v.at[h].reshape(256, 128)[pl.ds(i + j, NZ, stride=32), :] = new[j, :, 128 * h : 128 * h + 128]
        return c

    for n in range(4):
        last(n, 0)
        for h in range(2):
            rows, cols = pl.ds(8 * n, 8), pl.ds(128 * h, 128)
            pltpu.make_async_copy(out_v.at[h, :, rows], field.at[:, rows, cols], store_sem.at[n, h]).start()

    grouped([n for n in transfers if n[0] in late], lambda c: c.wait_send(), 1)
    for n in range(4):
        for h in range(2):
            rows, cols = pl.ds(8 * n, 8), pl.ds(128 * h, 128)
            pltpu.make_async_copy(out_v.at[h, :, rows], field.at[:, rows, cols], store_sem.at[n, h]).wait()


def solution(mesh):
    gx, gy = mesh.shape["gx"], mesh.shape["gy"]
    def step(*args):
        scratch = [
            pltpu.VMEM((2, NZ, R0, 128), F32),
            pltpu.VMEM((2, 4, NZ, R0, 128), jnp.bfloat16),
            pltpu.VMEM((2, 4, NZ * R0, 128), F32),
            pltpu.VMEM((2, NZ, R0, 128), F32),
        ]
        for rows, cols in zip(ROWS, LANES):
            scratch.append(pltpu.VMEM((5, rows, NZ, cols), F32))
            scratch += [pltpu.VMEM((rows, NZ, cols), F32)] * 4
        scratch += [
            pltpu.VMEM((2, 1, 5, NZ, 128), F32),
            pltpu.VMEM((2, 1, 5, NZ, 128), F32),
            pltpu.VMEM((2, 2, NZ, 128), F32),
            pltpu.VMEM((2, 2, NZ, 128), F32),
            pltpu.VMEM((2, 1, 4, NZ, 128), F32),
            pltpu.VMEM((2, 3, 1, 4, NZ, 128), F32),
            pltpu.VMEM((2, 1, NZ, 128), F32),
            pltpu.VMEM((2, 3, 1, NZ, 128), F32),
            pltpu.VMEM((NZ, 128), F32),
            pltpu.VMEM((3, 3, NZ, 128), F32),
            pltpu.VMEM((4, NZ, 128), F32),
            pltpu.VMEM((3, 3, 4, NZ, 128), F32),
            pltpu.VMEM((4, 2, NZ, 128), F32),
            pltpu.VMEM((3, 3, 4, 2, NZ, 128), F32),
            pltpu.VMEM((2 * REACH + 1, NZ, 128), F32),
            pltpu.VMEM((2, 2 * REACH + 1, NZ, 128), F32),
            pltpu.VMEM((3, NZ, 128), F32),
            pltpu.VMEM((2 * REACH, NZ, 128), F32),
            pltpu.VMEM((2, 2, NZ, 128), F32),
            pltpu.SemaphoreType.DMA((2, 5)),
            pltpu.SemaphoreType.DMA((4, 2)),
            pltpu.SemaphoreType.DMA((NSEM,)),
            pltpu.SemaphoreType.DMA((NSEM,)),
            pltpu.SemaphoreType.REGULAR((3, 2)),
        ]

        def body(*refs):
            kernel(gx, gy, *refs)

        return pl.pallas_call(
            body,
            out_shape=jax.ShapeDtypeStruct((NZ, R0, C0), F32),
            in_specs=[pl.BlockSpec(memory_space=pl.ANY)] * 5,
            out_specs=pl.BlockSpec(memory_space=pl.ANY),
            scratch_shapes=scratch,
            compiler_params=pltpu.CompilerParams(
                collective_id=0, has_side_effects=True, vmem_limit_bytes=60 * 2**20
            ),
        )(*args)

    placed = P(None, "gx", "gy")
    return jax.shard_map(step, mesh=mesh, in_specs=(placed,) * 5, out_specs=placed, check_vma=False)
```

```python
import jax
import jax.numpy as jnp
from jax import lax
from jax.experimental import pallas as pl
from jax.experimental.pallas import tpu as pltpu
from jax.sharding import PartitionSpec as P

DAMPING = 0.8
F32 = jnp.float32
MESH = pl.DeviceIdType.MESH
NZ, R0, C0 = 8, 32, 256
OWN = (4, 8, 8, 4, 12, 6)
ROWS = (40, 32, 24, 12, 26, 12)
LANES = (384, 256, 128, 128, 128, 128)
REACH = 6
NSEM = 96
AROUND = [(dx, dy) for dx in (0, 1, -1) for dy in (0, 1, -1) if dx or dy]


def lanes_of(shape):
    return lax.broadcasted_iota(jnp.int32, shape, len(shape) - 1)


def left(values):
    return pltpu.roll(values, values.shape[-1] - 1, values.ndim - 1)


def right(values):
    return pltpu.roll(values, 1, values.ndim - 1)


def above(values):
    return pltpu.roll(values, values.shape[-2] - 1, values.ndim - 2)


def below(values):
    return pltpu.roll(values, 1, values.ndim - 2)


def take(values, index):
    rows = values.size // 128
    flat = jnp.take_along_axis(values.reshape(rows, 128), jnp.broadcast_to(index, (rows, 128)), axis=1)
    return flat.reshape(values.shape)


def squeeze(first, second, odd=False):
    lane = lanes_of((1, 128))
    index = (2 * lane + (1 if odd else 0)) & 127
    one = take(first, index)
    if second is None:
        return one
    return jnp.where(lanes_of(first.shape) < 64, one, take(second, index))


def pair(values):
    return values + pltpu.roll(values, 127, values.ndim - 1)


def squeeze_wide(values, odd=False, sums=True):
    parts = [values[..., 128 * j : 128 * j + 128] for j in range(values.shape[-1] // 128)]
    if sums:
        parts = [pair(p) for p in parts]
    return squeeze(parts[0], parts[1] if len(parts) > 1 else None, odd)


def stretch_index(kind):
    lane = lanes_of((1, 128))
    half = lane // 2
    if kind == "low":
        return half
    if kind == "high":
        return half + 64
    split = 64 if kind == "ends" else 96
    return half + jnp.where(lane >= split, 64, 0)


def chunks(lo, hi, step, body):
    for i in range(lo, hi, step):
        body(i, min(step, hi - i))


class Level:
    def __init__(self, level, a, d, rd, va, vb):
        self.level, self.a, self.d, self.rd, self.va, self.vb = level, a, d, rd, va, vb
        self.own = OWN[level]
        self.step = (38, 32, 24, 12, 26, 12)[level]

    def rows(self, ref, i, k):
        return ref[pl.ds(i + self.own, k)]

    def field(self, f, i, k):
        return self.a[f, pl.ds(i + self.own, k)]

    def diagonal(self, lo, hi):
        def body(i, k):
            kappa = self.field(1, i, k)
            fx, fxl, fy, fz = self.field(2, i, k), self.field(2, i - 1, k), self.field(3, i, k), self.field(4, i, k)
            d = kappa + fx + fxl + fy + right(fy) + fz + below(fz)
            self.d[pl.ds(i + self.own, k)] = d
            self.rd[pl.ds(i + self.own, k)] = jnp.where(kappa > 0, DAMPING / d, 0.0)

        chunks(lo, hi, self.step, body)

    def beside(self, v, i, k):
        c = self.rows(v, i, k)
        fx, fxl, fy, fz = self.field(2, i, k), self.field(2, i - 1, k), self.field(3, i, k), self.field(4, i, k)
        along_x = fx * self.rows(v, i + 1, k) + fxl * self.rows(v, i - 1, k)
        along_y = fy * left(c) + right(fy * c)
        along_z = fz * above(c) + below(fz * c)
        return c, (self.field(0, i, k) + along_x) + (along_y + along_z)

    def first(self, lo, hi, out):
        def body(i, k):
            out[pl.ds(i + self.own, k)] = self.rows(self.rd, i, k) * self.field(0, i, k)

        chunks(lo, hi, self.step, body)

    def sweep(self, lo, hi, v, out):
        def body(i, k):
            c, total = self.beside(v, i, k)
            new = (1 - DAMPING) * c + self.rows(self.rd, i, k) * total
            out[pl.ds(i + self.own, k)] = new

        chunks(lo, hi, self.step, body)

    def beside_values(self, v, lo):
        c, k = v[1:-1], v.shape[0] - 2
        fx, fxl, fy, fz = self.field(2, lo, k), self.field(2, lo - 1, k), self.field(3, lo, k), self.field(4, lo, k)
        along_x = fx * v[2:] + fxl * v[:-2]
        along_y = fy * left(c) + right(fy * c)
        along_z = fz * above(c) + below(fz * c)
        return c, (self.field(0, lo, k) + along_x) + (along_y + along_z)

    def first_values(self, lo, hi):
        return self.rows(self.rd, lo, hi - lo) * self.field(0, lo, hi - lo)

    def sweep_values(self, v, lo):
        c, total = self.beside_values(v, lo)
        return (1 - DAMPING) * c + self.rows(self.rd, lo, c.shape[0]) * total

    def down(self, lo, hi, v, coarse):
        v = self.sweep_values(v, lo + 1)
        self.vb[pl.ds(lo + 1 + self.own, v.shape[0])] = v
        c, total = self.beside_values(v, lo + 2)
        residual = total - self.rows(self.d, lo + 2, c.shape[0]) * c
        m = c.shape[0] // 2
        residual = residual.reshape(m, 2, *residual.shape[1:])
        coarse.a[0, pl.ds((lo + 2) // 2 + coarse.own, m)] = squeeze_wide(residual[:, 0] + residual[:, 1]) * 0.25

    def up(self, v, lo, hi, cut=0):
        m = v.shape[0]
        if self.level == 1:
            parts = [take(v, stretch_index("low")), take(v, stretch_index("high"))]
        else:
            parts = [take(v, stretch_index("late"))]
        parts = [jnp.broadcast_to(p[:, None], (m, 2, NZ, 128)).reshape(2 * m, NZ, 128) for p in parts]
        v = self.rows(self.vb, lo, hi - lo) + (parts[0] if len(parts) == 1 else jnp.concatenate(parts, axis=2))
        v = v[cut : v.shape[0] - cut]
        return self.sweep_values(self.sweep_values(v, lo + cut + 1), lo + cut + 2)

    def restrict_residual(self, lo, hi, v, coarse):
        def body(n, m):
            k = 2 * m
            i = 2 * n
            c, total = self.beside(v, i, k)
            residual = total - self.rows(self.d, i, k) * c
            residual = residual[..., : min(residual.shape[-1], 256)]
            residual = residual.reshape(m, 2, *residual.shape[1:])
            coarse.a[0, pl.ds(n + coarse.own, m)] = fit(squeeze_wide(residual[:, 0] + residual[:, 1]) * 0.25, coarse)

        chunks(lo // 2, hi // 2, self.step // 2, body)

    def coarsen(self, lo, hi, coarse, fx_low=None):
        def body(n, m):
            both = [self.field(f, 2 * n, 2 * m)[..., : min(self.a.shape[-1], 256)] for f in (1, 2, 3, 4)]
            both = [b.reshape(m, 2, *b.shape[1:]) for b in both]
            kappa, fx, fy, fz = both
            at = pl.ds(n + coarse.own, m)
            coarse.a[1, at] = fit(squeeze_wide(kappa[:, 0] + kappa[:, 1]) * 0.25, coarse)
            coarse.a[2, at] = fit(squeeze_wide(fx[:, 1]) * 0.25, coarse)
            coarse.a[3, at] = fit(squeeze_wide(fy[:, 0] + fy[:, 1], odd=True, sums=False) * 0.25, coarse)
            coarse.a[4, at] = fit(squeeze_wide(fz[:, 0] + fz[:, 1]) * 0.25, coarse)

        chunks(lo, hi, self.step // 2, body)
        if fx_low is not None:
            fx = self.field(2, 2 * fx_low + 1, 1)
            coarse.a[2, pl.ds(fx_low + coarse.own, 1)] = squeeze_wide(fx) * 0.25

    def correct(self, lo, hi, v, coarse, c, out):
        def body(n, m):
            values = c[pl.ds(n + coarse.own, m)]
            if self.level == 0:
                first, second = values[..., :128], values[..., 128:]
                fine = [take(first, stretch_index("low")), take(first, stretch_index("high")), take(second, stretch_index("ends"))]
            elif self.level == 1:
                fine = [take(values, stretch_index("low")), take(values, stretch_index("high"))]
            else:
                fine = [take(values, stretch_index("late"))]
            for j, part in enumerate(fine):
                cols = slice(128 * j, 128 * j + 128)
                at = pl.ds(2 * n + self.own, 2 * m)
                spread = jnp.broadcast_to(part[:, None], (m, 2, NZ, 128)).reshape(2 * m, NZ, 128)
                out[at, :, cols] = v[at, :, cols] + spread

        chunks(lo // 2, hi // 2, max(self.step // 2, 1), body)


def fit(values, coarse):
    if coarse.level == 1:
        return jnp.concatenate([values, jnp.zeros_like(values)], axis=-1)
    return values


def kernel(gx, gy, source, kappa_sq, face_x, face_y, face_z, field, *refs):
    refs = list(refs)

    def get(n):
        out = refs[:n]
        del refs[:n]
        return out

    raw_s, raw_c, wide, out_v = get(4)
    levels = []
    for n in range(6):
        levels.append(Level(n, *get(5)))
    send0, recv0, corner, recvc, send1, recv1, sendr, recvr = get(8)
    send3, recv3, sendk, recvk, send2, recv2 = get(6)
    pack4, side4, widev, recvvx, recv3x = get(5)
    load_sem, store_sem, ssem, rsem, known = get(5)
    l0, l1, l2, l3, l4, l5 = levels

    mx, my = lax.axis_index("gx"), lax.axis_index("gy")

    def there(dx):
        if dx == 0:
            return None
        return mx + dx < gx if dx > 0 else mx + dx >= 0

    def when(cond, action):
        if cond is None:
            action()
        else:
            pl.when(cond)(action)

    far = [s * k for k in range(REACH, 0, -1) for s in (1, -1)]

    barrier = pltpu.get_barrier_semaphore()
    partners = AROUND
    count = 0
    for dx in (0, 1, -1):
        group = [p for p in partners if p[0] == dx]

        def greet(group=group):
            for px, py in group:
                ids = (mx + px, lax.rem(my + py + gy, gy))
                pl.semaphore_signal(barrier, inc=1, device_id=ids, device_id_type=MESH)

        when(there(dx), greet)
        count = count + (len(group) if dx == 0 else jnp.where(there(dx), len(group), 0))

    loads = []
    for h in range(2):
        cols = pl.ds(128 * h, 128)
        loads.append(pltpu.make_async_copy(source.at[:, :, cols], raw_s.at[h], load_sem.at[h, 0]))
        for f, ref in enumerate((kappa_sq, face_x, face_y, face_z)):
            loads.append(pltpu.make_async_copy(ref.at[:, :, cols], raw_c.at[h, f], load_sem.at[h, f + 1]))
    for copy in loads:
        copy.start()

    transfers = {}

    def plan(name, src, dst, dx, dy):
        transfers[name] = (src, dst, dx, dy, len(transfers))

    def copy_of(name):
        src, dst, dx, dy, n = transfers[name]
        ids = (mx + dx, lax.rem(my + dy + gy, gy))
        return pltpu.make_async_remote_copy(
            src_ref=src, dst_ref=dst, send_sem=ssem.at[n], recv_sem=rsem.at[n], device_id=ids, device_id_type=MESH
        )

    def grouped(names, action, sign):
        by = {}
        for name in names:
            by.setdefault(transfers[name][2], []).append(name)
        reach = max(abs(dx) for dx in by)

        def group(dx):
            for name in by[dx]:
                action(copy_of(name))

        def every():
            for dx in by:
                group(dx)

        def some():
            for dx in by:
                when(there(sign * dx), lambda dx=dx: group(dx))

        if reach == 0:
            every()
        else:
            inside = (mx >= reach) & (mx < gx - reach)
            pl.when(inside)(every)
            pl.when(jnp.logical_not(inside))(some)

    def send(names):
        grouped(names, lambda c: c.start(), 1)

    def arrive(names):
        grouped(names, lambda c: c.wait_recv(), -1)

    a0, a1 = l0.a, l1.a
    cols, cols1 = pl.ds(0, C0), pl.ds(0, 128)

    def rows0(name, fields, src, dst, rows, d):
        plan((name, d), a0.at[fields, pl.ds(src, rows), :, cols], a0.at[fields, pl.ds(dst, rows), :, cols], d, 0)

    rows0("x0", pl.ds(0, 5), 34, 2, 2, 1)
    rows0("x0f", 2, 33, 1, 1, 1)
    rows0("x0", pl.ds(0, 5), 4, 36, 2, -1)
    rows0("x0b", pl.ds(0, 2), 33, 1, 1, 1)
    rows0("x0c", pl.ds(3, 2), 33, 1, 1, 1)
    rows0("x0d", 2, 32, 0, 1, 1)
    rows0("x0b", pl.ds(0, 5), 6, 38, 1, -1)
    for d, src, dst, n1, nr in ((1, 24, 8, 7, 6), (-1, 8, 24, 6, 6)):
        for name, fields, n in (("x1", pl.ds(1, 4), n1), ("xr", 0, nr)):
            s_at, d_at = (pl.ds(src - n, n), pl.ds(dst - n, n)) if d == 1 else (pl.ds(src, n), pl.ds(dst, n))
            plan((name, d), a1.at[fields, s_at, :, cols1], a1.at[fields, d_at, :, cols1], d, 0)
    for dx, dy in AROUND:
        e = (dy + 1) // 2
        if dy and dx == 0:
            plan(("y0", dx, dy), send0.at[e], recv0.at[e], dx, dy)
        if dy and dx:
            plan(("c0", dx, dy), corner.at[e, (dx + 1) // 2], recvc.at[e, (dx + 1) // 2], dx, dy)
        if dy:
            plan(("y1", dx, dy), send1.at[e], recv1.at[e, dx + 1], dx, dy)
            plan(("yr", dx, dy), sendr.at[e], recvr.at[e, dx + 1], dx, dy)
        plan(("k3", dx, dy), sendk, recvk.at[dx + 1, dy + 1], dx, dy)
        plan(("r3", dx, dy), send3, recv3.at[dx + 1, dy + 1], dx, dy)
        pairs = pl.ds(2 if dx == 1 else 0, 2 if dx else 4)
        plan(("e2", dx, dy), send2.at[pairs], recv2.at[dx + 1, dy + 1, pairs], dx, dy)
    for dy in (1, -1):
        plan(("y4", dy), pack4, side4.at[(dy + 1) // 2], 0, dy)
    for n, dx in enumerate(far):
        plan(("x4", dx), pack4.at[2 * REACH], pack4.at[n], dx, 0)
        plan(("xv", dx), widev.at[0], recvvx.at[n], dx, 0)
    for n, dx in enumerate((1, -1)):
        plan(("x3", dx), widev.at[pl.ds(1, 2)], recv3x.at[n], dx, 0)
    assert len(transfers) <= NSEM

    def tell(word):
        for e, dx in enumerate((1, -1) if word == 0 else (2, -2)):

            def go(e=e, dx=dx):
                pl.semaphore_signal(known.at[word, e], inc=1, device_id=(mx + dx, my), device_id_type=MESH)

            when(there(dx), go)

    def hear(word):
        for e, dx in enumerate((1, -1) if word == 0 else (2, -2)):
            when(there(-dx), lambda e=e: pl.semaphore_wait(known.at[word, e], 1))

    def zero(ref, *index):
        ref[index] = jnp.zeros(ref[index].shape, F32)

    @pl.when(mx == 0)
    def _():
        l0.a[:, 0:4] = jnp.zeros((5, 4, NZ, 384), F32)
        l1.a[:, 0:8] = jnp.zeros((5, 8, NZ, 256), F32)
        recv3x[0] = jnp.zeros((2, NZ, 128), F32)

    @pl.when(mx == gx - 1)
    def _():
        l0.a[:, 36:40] = jnp.zeros((5, 4, NZ, 384), F32)
        l1.a[:, 24:32] = jnp.zeros((5, 8, NZ, 256), F32)
        recv3x[1] = jnp.zeros((2, NZ, 128), F32)

    for n, dx in enumerate(far):

        @pl.when(jnp.logical_not(there(-dx)))
        def _(n=n):
            pack4[n] = jnp.zeros((NZ, 128), F32)
            recvvx[n] = jnp.zeros((NZ, 128), F32)

    for copy in loads:
        copy.wait()

    def widen(h, c):
        for f in range(4):
            wide[h, f] = raw_c[h, f].reshape(256, 128).astype(F32)
        top = pl.ds(224, 32)
        wide[h, 0, top] = wide[h, 0, top] + wide[h, 3, top]
        wide[h, 3, top] = jnp.zeros((32, 128), F32)
        return c

    for h in range(2):
        widen(h, 0)

    def turn(i):
        for h in range(2):
            cols = slice(128 * h, 128 * h + 128)
            l0.a[0, 4 + i, :, cols] = raw_s.at[h].reshape(256, 128)[pl.ds(i, NZ, stride=32), :]
            for f in range(4):
                l0.a[1 + f, 4 + i, :, cols] = wide.at[h, f][pl.ds(i, NZ, stride=32), :]

    for i in range(R0):
        turn(i)

    def pack(a, fields, own, count, width, last, dst):
        per = 128 // width
        lane = lanes_of((NZ, 128))
        for e in range(2):
            at = pl.ds(last, 128) if e == 1 else pl.ds(0, 128)
            for g in range(count // per):
                total = None
                for j in range(per):
                    row = a[fields, own + g * per + j, :, at]
                    shift = (width * j + (width if e == 1 else 0)) % 128
                    row = pltpu.roll(row, shift, row.ndim - 1) if shift else row
                    total = row if total is None else jnp.where(lane // width == j, row, total)
                dst[e, g] = total

    has_left, has_right = my > 0, my < gy - 1

    def unpack(part, a, fields, own, count, width, last, rows):
        lane = lanes_of((NZ, 128))
        for i in rows:
            dx = -1 if i < 0 else (1 if i >= count else 0)
            keep_r, keep_l = has_right, has_left
            if dx:
                keep_r, keep_l = keep_r & there(dx), keep_l & there(dx)
            sides = []
            for e in range(2):
                values, place = part(e, dx, i - dx * count)
                shift = (128 - width * (place + e)) % 128
                sides.append(pltpu.roll(values, shift, values.ndim - 1) if shift else values)
            row = jnp.where((lane < width) & keep_r, sides[0], jnp.where((lane >= 128 - width) & keep_l, sides[1], 0.0))
            a[fields, own + i, :, pl.ds(last, 128)] = row

    all_fields, coefs = slice(0, 5), slice(1, 5)
    lane = lanes_of((NZ, 128))
    sides = [p for p in AROUND if p[1]]

    def names(name, places=AROUND):
        return [(name, *p) for p in places]

    first = [("x0", 1), ("x0f", 1), ("x0", -1)] + names("y0", [(0, 1), (0, -1)]) + names("c0", [p for p in sides if p[0]])
    pl.semaphore_wait(barrier, count)
    send(first[:3])
    pack(l0.a, all_fields, 4, 32, 4, 128, send0)
    for e in range(2):
        for d in range(2):
            total = None
            for f in range(5):
                shift = (16 * f - (112 if d else 0)) % 128
                part = send0[e, 0, f]
                part = pltpu.roll(part, shift, 1) if shift else part
                total = part if total is None else jnp.where(lane < 16 * f, total, part)
            corner[e, d] = total
    first = [("x0", 1), ("x0f", 1), ("x0", -1)] + names("y0", [(0, 1), (0, -1)]) + names("c0", [p for p in sides if p[0]])
    send(first[3:])
    l0.coarsen(0, 16, l1)
    pack(l1.a, coefs, 8, 16, 8, 0, send1)

    second = [("x1", 1), ("x1", -1)] + names("y1", sides)
    send(second)
    tell(0)
    l1.coarsen(0, 8, l2)
    l2.coarsen(0, 4, l3)

    def pack3(row):
        total = row(0)
        for j in range(1, 4):
            part = row(j)
            total = jnp.where(lane < 32 * j, total, pltpu.roll(part, 32 * j, part.ndim - 1))
        return total

    sendk[...] = pack3(lambda j: l3.a[1:5, 4 + j])
    send(names("k3"))
    l3.coarsen(0, 2, l4)
    total = l4.a[1, 12]
    for q in range(1, 8):
        total = jnp.where(lane < 16 * q, total, pltpu.roll(l4.a[1 + q // 2, 12 + q % 2], 16 * q, 1))
    pack4[2 * REACH] = total

    def part0(e, dx, j):
        if dx == 0:
            return recv0[e, 0], j
        j = j - 28 if dx < 0 else j
        values = recvc[e, (1 - dx) // 2]
        return jnp.stack([pltpu.roll(values, 128 - 16 * f, 1) if f else values for f in range(5)]), j

    beside = first[3:5]
    hear(0)
    tell(1)
    arrive(beside)
    unpack(part0, l0.a, all_fields, 4, 32, 4, 256, range(32))
    l0.diagonal(1, 32)
    l0.first(1, 32, l0.va)
    l0.sweep(2, 31, l0.va, l0.vb)
    l0.restrict_residual(4, 30, l0.vb, l1)
    close = names("y1", [(0, 1), (0, -1)])
    hear(1)
    tell(2)
    arrive(first[:3] + first[5:])
    unpack(part0, l0.a, all_fields, 4, 32, 4, 256, [*range(-4, 0), *range(32, 35)])
    for lo, hi in ((-2, 1), (32, 34)):
        l0.diagonal(lo, hi)
    for lo, hi in ((-2, 1), (32, 34)):
        l0.first(lo, hi, l0.va)
    for lo, hi in ((-1, 2), (31, 33)):
        l0.sweep(lo, hi, l0.va, l0.vb)
    for lo, hi in ((0, 4), (30, 32)):
        l0.restrict_residual(lo, hi, l0.vb, l1)
    third = [("xr", 1), ("xr", -1)] + names("yr", sides)
    send(third[:2])
    pack(l1.a, 0, 8, 16, 8, 0, sendr)
    send(third[2:])
    arrive(close)

    def part1(e, dx, j):
        return recv1[e, 1 - dx, 0], j

    unpack(part1, l1.a, coefs, 8, 16, 8, 128, range(16))
    l1.diagonal(1, 16)
    later = [("x0b", 1), ("x0c", 1), ("x0d", 1), ("x0b", -1)]

    arrive([n for n in second if n not in close])
    unpack(part1, l1.a, coefs, 8, 16, 8, 128, [*range(-7, 0), *range(16, 22)])
    l1.diagonal(-6, 1)
    l1.diagonal(16, 22)
    l1.coarsen(-3, 11, l2, fx_low=-4)
    l2.diagonal(-3, 11)

    def spread3(own, src, a, fields):
        for px in (-1, 0, 1):
            mid, from_r, from_l = own if px == 0 else src[1 - px, 1], src[1 - px, 0], src[1 - px, 2]
            for j in range(4):
                parts = []
                for values, shift in ((mid, -32 * j), (from_r, 32 - 32 * j), (from_l, 96 - 32 * j)):
                    parts.append(pltpu.roll(values, shift % 128, values.ndim - 1) if shift % 128 else values)
                row = jnp.where((lane < 64) & has_right, parts[1], jnp.where((lane >= 96) & has_left, parts[2], 0.0))
                row = jnp.where(lane < 32, parts[0], row)
                if px:
                    row = jnp.where(there(px), row, 0.0)
                a[fields, 4 + 4 * px + j] = row

    hear(2)
    send([("x4", dx) for dx in far])
    arrive(third)
    unpack(lambda e, dx, j: (recvr[e, 1 - dx, 0], j), l1.a, 0, 8, 16, 8, 128, range(-6, 22))
    l1.down(-6, 22, l1.first_values(-6, 22), l2)
    l2.down(-2, 10, l2.first_values(-2, 10), l3)

    send3[...] = pack3(lambda j: l3.a[0, 4 + j])
    send(names("r3"))
    for n in range(4):
        send2[n, 0] = jnp.where(lane < 64, l2.a[0, 8 + 2 * n], pltpu.roll(l2.a[0, 9 + 2 * n], 64, 1))
        send2[n, 1] = jnp.where(lane < 64, l2.vb[8 + 2 * n], pltpu.roll(l2.vb[9 + 2 * n], 64, 1))
    send(names("e2"))
    send(later)
    arrive(names("k3"))
    spread3(sendk[...], recvk, l3.a, coefs)
    l3.diagonal(-3, 7)
    l3.coarsen(-1, 2, l4)
    l4.diagonal(0, 2)

    arrive(names("r3"))
    spread3(send3[...], recv3, l3.a, 0)
    l3.down(-2, 6, l3.first_values(-2, 6), l4)
    l4.first(0, 2, l4.va)

    def two(ref, i):
        return jnp.where((lane < 48) | (lane >= 112), ref[i], pltpu.roll(ref[i + 1], 64, 1))

    widev[0] = two(l4.va, 12)
    send([("xv", dx) for dx in far])
    for n in range(2):
        widev[1 + n] = two(l3.vb, 4 + 2 * n)
    send([("x3", 1), ("x3", -1)])

    def spread_two(both, ref, i):
        ref[i] = both
        ref[i + 1] = pltpu.roll(both, 64, both.ndim - 1)

    arrive([("x4", dx) for dx in far])
    send([("y4", 1), ("y4", -1)])

    arrive(later)
    for lo, hi in ((-3, -2), (34, 35)):
        l0.diagonal(lo, hi)
        l0.first(lo, hi, l0.va)
    for lo, hi in ((-2, -1), (33, 34)):
        l0.sweep(lo, hi, l0.va, l0.vb)
    arrive(names("e2"))
    for px in (-1, 0, 1):
        for n in (range(2, 4) if px < 0 else range(2) if px else range(4)):
            mid = send2[n] if px == 0 else recv2[1 - px, 1, n]
            from_r, from_l = recv2[1 - px, 0, n], recv2[1 - px, 2, n]
            zero = jnp.zeros_like(mid)
            from_r, from_l = jnp.where(has_right, from_r, zero), jnp.where(has_left, from_l, zero)
            even = jnp.where(lane < 64, mid, pltpu.roll(jnp.where(lane < 32, from_r, from_l), 64, 2))
            odd = jnp.where(lane < 64, pltpu.roll(mid, 64, 2), jnp.where(lane < 96, from_r, from_l))
            for j, row in enumerate((even, odd)):
                if px:
                    row = jnp.where(there(px), row, zero)
                i = 8 + 8 * px + 2 * n + j
                l2.a[0, i] = row[0]
                l2.vb[i] = row[1]

    late = ("xv", "x3", "x4", "y4")
    grouped([n for n in transfers if n[0] not in late], lambda c: c.wait_send(), 1)
    arrive([("y4", 1), ("y4", -1)])
    keep_r, keep_l = (lane < 64) & has_right, (lane >= 64) & has_left
    for n, dx in enumerate(far + [0]):
        i = 12 - 2 * dx
        own, from_r, from_l = pack4[n], side4[0, n], side4[1, n]
        for q in range(8):
            parts = [pltpu.roll(p, b % 128, 1) if b % 128 else p for p, b in ((own, -16 * q), (from_r, 16 - 16 * q), (from_l, -16 - 16 * q))]
            row = jnp.where(lane < 16, parts[0], jnp.where(keep_r, parts[1], jnp.where(keep_l, parts[2], 0.0)))
            l4.a[1 + q // 2, i + q % 2] = row
    l4.diagonal(-11, 13)
    l4.coarsen(-5, 6, l5, fx_low=-6)
    l5.diagonal(-5, 6)

    arrive([("xv", dx) for dx in far])
    for n, dx in list(enumerate(far)) + [(None, 0)]:
        spread_two(widev[0] if dx == 0 else recvvx[n], l4.va, 12 - 2 * dx)

    v = l4.rows(l4.va, -12, 26)
    l4.a[0, pl.ds(1, 24)] = v[1:25] * l4.rows(l4.d, -11, 24) * (1 / DAMPING)
    l4.down(-12, 14, v, l5)

    v = l5.first_values(-5, 6)
    for lo in (-4, -3, -2):
        v = l5.sweep_values(v, lo)

    v = l4.up(v, -4, 6)
    arrive([("x3", 1), ("x3", -1)])
    for src, dx in ((recv3x.at[0], 1), (recv3x.at[1], -1)):
        for n in range(2):
            spread_two(src[n], l3.vb, 4 - 4 * dx + 2 * n)
    v = l3.up(v, -4, 8)
    v = l2.up(v, -4, 12)
    l1.va[pl.ds(l1.own - 1, 18)] = l1.up(v, -4, 20, 1)

    l0.correct(-2, 34, l0.vb, l1, l1.va, l0.va)
    l0.sweep(-1, 33, l0.va, l0.vb)

    def last(n, c):
        for q in range(2):
            i = 8 * n + 4 * q
            mid, total = l0.beside(l0.vb, i, 4)
            new = (1 - DAMPING) * mid + l0.rows(l0.rd, i, 4) * total
            for j in range(4):
                for h in range(2):
                    out_v.at[h].reshape(256, 128)[pl.ds(i + j, NZ, stride=32), :] = new[j, :, 128 * h : 128 * h + 128]
        return c

    for n in range(4):
        last(n, 0)
        for h in range(2):
            rows, cols = pl.ds(8 * n, 8), pl.ds(128 * h, 128)
            pltpu.make_async_copy(out_v.at[h, :, rows], field.at[:, rows, cols], store_sem.at[n, h]).start()

    grouped([n for n in transfers if n[0] in late], lambda c: c.wait_send(), 1)
    for n in range(4):
        for h in range(2):
            rows, cols = pl.ds(8 * n, 8), pl.ds(128 * h, 128)
            pltpu.make_async_copy(out_v.at[h, :, rows], field.at[:, rows, cols], store_sem.at[n, h]).wait()


def solution(mesh):
    gx, gy = mesh.shape["gx"], mesh.shape["gy"]
    def step(*args):
        scratch = [
            pltpu.VMEM((2, NZ, R0, 128), F32),
            pltpu.VMEM((2, 4, NZ, R0, 128), jnp.bfloat16),
            pltpu.VMEM((2, 4, NZ * R0, 128), F32),
            pltpu.VMEM((2, NZ, R0, 128), F32),
        ]
        for rows, cols in zip(ROWS, LANES):
            scratch.append(pltpu.VMEM((5, rows, NZ, cols), F32))
            scratch += [pltpu.VMEM((rows, NZ, cols), F32)] * 4
        scratch += [
            pltpu.VMEM((2, 1, 5, NZ, 128), F32),
            pltpu.VMEM((2, 1, 5, NZ, 128), F32),
            pltpu.VMEM((2, 2, NZ, 128), F32),
            pltpu.VMEM((2, 2, NZ, 128), F32),
            pltpu.VMEM((2, 1, 4, NZ, 128), F32),
            pltpu.VMEM((2, 3, 1, 4, NZ, 128), F32),
            pltpu.VMEM((2, 1, NZ, 128), F32),
            pltpu.VMEM((2, 3, 1, NZ, 128), F32),
            pltpu.VMEM((NZ, 128), F32),
            pltpu.VMEM((3, 3, NZ, 128), F32),
            pltpu.VMEM((4, NZ, 128), F32),
            pltpu.VMEM((3, 3, 4, NZ, 128), F32),
            pltpu.VMEM((4, 2, NZ, 128), F32),
            pltpu.VMEM((3, 3, 4, 2, NZ, 128), F32),
            pltpu.VMEM((2 * REACH + 1, NZ, 128), F32),
            pltpu.VMEM((2, 2 * REACH + 1, NZ, 128), F32),
            pltpu.VMEM((3, NZ, 128), F32),
            pltpu.VMEM((2 * REACH, NZ, 128), F32),
            pltpu.VMEM((2, 2, NZ, 128), F32),
            pltpu.SemaphoreType.DMA((2, 5)),
            pltpu.SemaphoreType.DMA((4, 2)),
            pltpu.SemaphoreType.DMA((NSEM,)),
            pltpu.SemaphoreType.DMA((NSEM,)),
            pltpu.SemaphoreType.REGULAR((3, 2)),
        ]

        def body(*refs):
            kernel(gx, gy, *refs)

        return pl.pallas_call(
            body,
            out_shape=jax.ShapeDtypeStruct((NZ, R0, C0), F32),
            in_specs=[pl.BlockSpec(memory_space=pl.ANY)] * 5,
            out_specs=pl.BlockSpec(memory_space=pl.ANY),
            scratch_shapes=scratch,
            compiler_params=pltpu.CompilerParams(
                collective_id=0, has_side_effects=True, vmem_limit_bytes=60 * 2**20
            ),
        )(*args)

    placed = P(None, "gx", "gy")
    return jax.shard_map(step, mesh=mesh, in_specs=(placed,) * 5, out_specs=placed, check_vma=False)
```
